512 devices in a mesh: dp: 16 (over y, core), dap: 32 (over x, z).
Axes of the slice: x: 4, y: 8, z: 8, core: 2. Of those that a mesh axis runs over, the one named last changes fastest.
Arguments:
- pair: bfloat16 [16, 256, 256, 128], P('dp', 'dap'), may hold values from -6 to 6
- cotangent: bfloat16 [16, 256, 256, 128], P('dp', 'dap'), may hold values from -6 to 6
- lengths: int32 [16], P('dp'), may hold values from 64 to 256, as said below
- w_in: bfloat16 [128, 640], replicated, may hold values from -0.5 to 0.5
- gain_in: float32 [128], replicated, may hold values from 0.5 to 1.5
- w_out: bfloat16 [128, 128], replicated, may hold values from -0.5 to 0.5
- gain_out: float32 [128], replicated, may hold values from 0.5 to 1.5
Outputs:
- pair_grad: bfloat16 [16, 256, 256, 128], P('dp', 'dap')
- w_in_grad: float32 [128, 640], replicated
- gain_in_grad: float32 [128], replicated
- w_out_grad: float32 [128, 128], replicated
- gain_out_grad: float32 [128], replicated
The draws below stay inside these ranges and needn't reach their ends.
Inputs may be any that keep to these rules, and one draw needn't show every extreme that they name: `lengths`: some complex has exactly 256 valid tokens and another exactly 64.
All inputs are finite; a program needn't handle non-finite values.
Results may differ from the reference program's by a relative error of at most 0.0095.
Values may be sent and summed in bfloat16 or wider, within the bound.
No kernel may reach another device: no remote copies, remote signals or barrier semaphores. Data moves between devices by JAX's collectives and lax.ppermute only.
A program may use at most 64 MiB of HBM per device.

```python
import math
import jax
import jax.numpy as jnp
from jax import lax

C = 128
N = 256
COMPLEXES = 16


def draw_lengths(key, part):
    key = jax.random.fold_in(key, 11)
    key_base, key_top, key_low = jax.random.split(key, 3)
    counts = jax.random.randint(key_base, (COMPLEXES,), N // 4, N + 1)
    highest = jax.random.randint(key_top, (), 0, COMPLEXES)
    lowest = (highest + 1 + jax.random.randint(key_low, (), 0, COMPLEXES - 1)) % COMPLEXES
    counts = counts.at[highest].set(N).at[lowest].set(N // 4)
    return counts.astype(jnp.int32)


def levels(own_key, shape, cuts, least, high):
    factor_of, own = 1.0, jax.random.fold_in(own_key, 6)
    for axis_at, blocks in cuts:
        heights = jnp.exp(jax.random.uniform(jax.random.fold_in(own, axis_at), (blocks,), jnp.float32, least / len(cuts), high / len(cuts)))
        factor_of = factor_of * jnp.repeat(heights, shape[axis_at] // blocks).reshape([-1 if axis == axis_at else 1 for axis in range(len(shape))])
    return factor_of


def gaussian(rng, extent, deviation, most, cuts=(), held_as=jnp.bfloat16):
    values = jax.random.normal(rng, extent, jnp.float32) * deviation
    if len(cuts) > 0:
        values = levels(rng, extent, cuts, -0.22, 0.18) * values
    return jnp.clip(values, min=-most, max=most).astype(held_as)


def setup_inputs(seed: int = 0) -> dict:
    arg_keys = jax.random.split(jax.random.key(seed), 8)
    pair = gaussian(arg_keys[0], (COMPLEXES, N, N, C), 1.0, 6.0, ((0, 16), (1, 32)))
    cotangent = gaussian(arg_keys[1], (COMPLEXES, N, N, C), 1.0, 6.0, ((0, 16), (1, 32)))
    lengths = draw_lengths(jax.random.fold_in(arg_keys[7], 71), 0)
    w_in = gaussian(arg_keys[3], (C, 5 * C), C ** -0.5, 0.5)
    gain_in = jnp.clip(jax.random.uniform(arg_keys[4], (C,), jnp.float32, 0.5, 1.5), 0.5, 1.5)
    w_out = gaussian(arg_keys[5], (C, C), C ** -0.5, 0.5)
    gain_out = jnp.clip(jax.random.uniform(arg_keys[6], (C,), jnp.float32, 0.5, 1.5), 0.5, 1.5)
    return {"pair": pair, "cotangent": cotangent, "lengths": lengths, "w_in": w_in, "gain_in": gain_in, "w_out": w_out, "gain_out": gain_out}


EPSILON = 1e-05

def normalize(values):
    centred = values - lax.optimization_barrier(jnp.mean(values, axis=-1, keepdims=True))
    variance = lax.optimization_barrier(jnp.mean(centred * centred, axis=-1, keepdims=True))
    inverse = lax.rsqrt(variance + EPSILON)
    return (centred * inverse, inverse)

def normalize_back(upstream, normed, inverse):
    first_mean = lax.optimization_barrier(jnp.mean(upstream, axis=-1, keepdims=True))
    second_mean = lax.optimization_barrier(jnp.mean(upstream * normed, axis=-1, keepdims=True))
    return inverse * (upstream - first_mean - normed * second_mean)

def column_block(weights, index, channels):
    return weights[:, index * channels:(index + 1) * channels]

def flat_product(first, second):
    return lax.dot_general(first.reshape(-1, first.shape[-1]), second.reshape(-1, second.shape[-1]), (((0,), (0,)), ((), ())), preferred_element_type=jnp.float32)

def project(pair, cell_mask, w_in, gain_in):
    channels = pair.shape[-1]
    pair_hat, pair_inverse = normalize(pair.astype(jnp.float32))
    pair_norm = (pair_hat * gain_in).astype(jnp.bfloat16)

    def linear(index):
        return jnp.dot(pair_norm, column_block(w_in, index, channels), preferred_element_type=jnp.float32)
    left_proj = linear(0)
    left_gate = jax.nn.sigmoid(linear(1))
    right_proj = linear(2)
    right_gate = jax.nn.sigmoid(linear(3))
    out_gate = jax.nn.sigmoid(linear(4))
    left = (cell_mask * left_gate * left_proj).astype(jnp.bfloat16)
    right = (cell_mask * right_gate * right_proj).astype(jnp.bfloat16)
    saved = (pair_hat, pair_inverse, pair_norm, left_proj, left_gate, right_proj, right_gate)
    return (saved, out_gate, left, right)

def output_backward(product, out_gate, cotangent, w_out, gain_out):
    prod_hat, prod_inverse = normalize(product.astype(jnp.float32))
    prod_norm = (prod_hat * gain_out).astype(jnp.bfloat16)
    update = jnp.dot(prod_norm, w_out, preferred_element_type=jnp.float32)
    upstream = cotangent.astype(jnp.float32)
    grad_update = (upstream * out_gate).astype(jnp.bfloat16)
    grad_gate = upstream * update * out_gate * (1.0 - out_gate)
    w_out_part = flat_product(prod_norm, grad_update)
    grad_norm = jnp.dot(grad_update, w_out.T, preferred_element_type=jnp.float32)
    gain_out_part = lax.optimization_barrier(jnp.sum((prod_hat * grad_norm).reshape(-1, prod_hat.shape[-1]), axis=0))
    grad_product = normalize_back(grad_norm * gain_out, prod_hat, prod_inverse).astype(jnp.bfloat16)
    return (grad_product, grad_gate, w_out_part, gain_out_part)

def input_backward(grad_left, grad_right, grad_gate, saved, cell_mask, w_in, gain_in):
    pair_hat, pair_inverse, pair_norm, left_proj, left_gate, right_proj, right_gate = saved
    channels = pair_hat.shape[-1]
    left_up = grad_left.astype(jnp.float32) * cell_mask
    right_up = grad_right.astype(jnp.float32) * cell_mask
    pieces = (left_up * left_gate, left_up * left_proj * left_gate * (1.0 - left_gate), right_up * right_gate, right_up * right_proj * right_gate * (1.0 - right_gate), grad_gate)
    pieces = [piece.astype(jnp.bfloat16) for piece in pieces]
    w_in_part = jnp.concatenate([flat_product(pair_norm, piece) for piece in pieces], axis=1)
    grad_norm = jnp.dot(pieces[0], column_block(w_in, 0, channels).T, preferred_element_type=jnp.float32)
    for index in range(1, 5):
        grad_norm = grad_norm + jnp.dot(pieces[index], column_block(w_in, index, channels).T, preferred_element_type=jnp.float32)
    gain_in_part = lax.optimization_barrier(jnp.sum((pair_hat * grad_norm).reshape(-1, channels), axis=0))
    grad_pair = normalize_back(grad_norm * gain_in, pair_hat, pair_inverse).astype(jnp.bfloat16)
    return (grad_pair, w_in_part, gain_in_part)

def reference(pair, cotangent, lengths, w_in, gain_in, w_out, gain_out):

    def one_complex(inputs):
        pair_one, cotangent_one, length_one = inputs
        token_ids = lax.iota(jnp.int32, pair_one.shape[1])
        token_mask = (token_ids[None, :] < length_one[:, None]).astype(jnp.float32)
        cell_mask = token_mask[:, :, None, None] * token_mask[:, None, :, None]
        saved, out_gate, left, right = project(pair_one, cell_mask, w_in, gain_in)
        product = jnp.einsum('bikc,bjkc->bijc', left.astype(jnp.float32), right.astype(jnp.float32)).astype(jnp.bfloat16)
        grad_product, grad_gate, w_out_part, gain_out_part = output_backward(product, out_gate, cotangent_one, w_out, gain_out)
        grad_wide = grad_product.astype(jnp.float32)
        grad_left = jnp.einsum('bijc,bjkc->bikc', grad_wide, right.astype(jnp.float32)).astype(jnp.bfloat16)
        grad_right = jnp.einsum('bijc,bikc->bjkc', grad_wide, left.astype(jnp.float32)).astype(jnp.bfloat16)
        grad_pair, w_in_part, gain_in_part = input_backward(grad_left, grad_right, grad_gate, saved, cell_mask, w_in, gain_in)
        return (grad_pair, w_in_part, gain_in_part, w_out_part, gain_out_part)
    results = lax.map(one_complex, (pair[:, None], cotangent[:, None], lengths[:, None]))
    factor = 1.0 / (N * math.sqrt(COMPLEXES))
    pair_grad = results[0][:, 0]
    w_in_grad = lax.optimization_barrier(jnp.sum(results[1], axis=0)) * factor
    gain_in_grad = lax.optimization_barrier(jnp.sum(results[2], axis=0)) * factor
    w_out_grad = lax.optimization_barrier(jnp.sum(results[3], axis=0)) * factor
    gain_out_grad = lax.optimization_barrier(jnp.sum(results[4], axis=0)) * factor
    return (pair_grad, w_in_grad, gain_in_grad, w_out_grad, gain_out_grad)
```

```python
import math

import jax
import jax.numpy as jnp
from jax import lax
from jax.sharding import PartitionSpec as P

EPSILON = 1e-05


def normalize(values):
    centred = values - jnp.mean(values, axis=-1, keepdims=True)
    variance = jnp.mean(centred * centred, axis=-1, keepdims=True)
    inverse = lax.rsqrt(variance + EPSILON)
    return (centred * inverse, inverse)


def normalize_back(upstream, normed, inverse):
    first_mean = jnp.mean(upstream, axis=-1, keepdims=True)
    second_mean = jnp.mean(upstream * normed, axis=-1, keepdims=True)
    return inverse * (upstream - first_mean - normed * second_mean)


def column_block(weights, index, channels):
    return weights[:, index * channels : (index + 1) * channels]


def flat_product(first, second):
    return lax.dot_general(
        first.reshape(-1, first.shape[-1]),
        second.reshape(-1, second.shape[-1]),
        (((0,), (0,)), ((), ())),
        preferred_element_type=jnp.float32,
    )


def channel_major(values):
    return jnp.transpose(values, (0, 3, 1, 2))


def channel_minor(values):
    return jnp.transpose(values, (0, 2, 3, 1))


def project(pair, cell_mask, w_in, gain_in):
    channels = pair.shape[-1]
    pair_hat, pair_inverse = normalize(pair.astype(jnp.float32))
    pair_norm = (pair_hat * gain_in).astype(jnp.bfloat16)

    def linear(index):
        return jnp.dot(
            pair_norm, column_block(w_in, index, channels), preferred_element_type=jnp.float32
        )

    left_proj = linear(0)
    left_gate = jax.nn.sigmoid(linear(1))
    right_proj = linear(2)
    right_gate = jax.nn.sigmoid(linear(3))
    out_gate = jax.nn.sigmoid(linear(4))
    left = (cell_mask * left_gate * left_proj).astype(jnp.bfloat16)
    right = (cell_mask * right_gate * right_proj).astype(jnp.bfloat16)
    saved = (pair_hat, pair_inverse, pair_norm, left_proj, left_gate, right_proj, right_gate)
    return (saved, out_gate, left, right)


def output_backward(product, out_gate, cotangent, w_out, gain_out):
    prod_hat, prod_inverse = normalize(product.astype(jnp.float32))
    prod_norm = (prod_hat * gain_out).astype(jnp.bfloat16)
    update = jnp.dot(prod_norm, w_out, preferred_element_type=jnp.float32)
    upstream = cotangent.astype(jnp.float32)
    grad_update = (upstream * out_gate).astype(jnp.bfloat16)
    grad_gate = upstream * update * out_gate * (1.0 - out_gate)
    w_out_part = flat_product(prod_norm, grad_update)
    grad_norm = jnp.dot(grad_update, w_out.T, preferred_element_type=jnp.float32)
    gain_out_part = jnp.sum((prod_hat * grad_norm).reshape(-1, prod_hat.shape[-1]), axis=0)
    grad_product = normalize_back(grad_norm * gain_out, prod_hat, prod_inverse).astype(jnp.bfloat16)
    return (grad_product, grad_gate, w_out_part, gain_out_part)


def input_backward(grad_left, grad_right, grad_gate, saved, cell_mask, w_in, gain_in):
    pair_hat, pair_inverse, pair_norm, left_proj, left_gate, right_proj, right_gate = saved
    channels = pair_hat.shape[-1]
    left_up = grad_left.astype(jnp.float32) * cell_mask
    right_up = grad_right.astype(jnp.float32) * cell_mask
    pieces = (
        left_up * left_gate,
        left_up * left_proj * left_gate * (1.0 - left_gate),
        right_up * right_gate,
        right_up * right_proj * right_gate * (1.0 - right_gate),
        grad_gate,
    )
    pieces = [piece.astype(jnp.bfloat16) for piece in pieces]
    w_in_part = jnp.concatenate([flat_product(pair_norm, piece) for piece in pieces], axis=1)
    grad_norm = jnp.dot(
        pieces[0], column_block(w_in, 0, channels).T, preferred_element_type=jnp.float32
    )
    for index in range(1, 5):
        grad_norm = grad_norm + jnp.dot(
            pieces[index], column_block(w_in, index, channels).T, preferred_element_type=jnp.float32
        )
    gain_in_part = jnp.sum((pair_hat * grad_norm).reshape(-1, channels), axis=0)
    grad_pair = normalize_back(grad_norm * gain_in, pair_hat, pair_inverse).astype(jnp.bfloat16)
    return (grad_pair, w_in_part, gain_in_part)


def exchange(values, axis):
    return lax.all_to_all(values, axis, split_axis=0, concat_axis=0, tiled=True)


def summed_everywhere(parts):
    inner, outer = lax.axis_size("dap"), lax.axis_size("dp")
    pieces = exchange(parts.reshape(inner, -1, 128), "dap")
    piece = jnp.sum(pieces, axis=0)
    pieces = exchange(jnp.broadcast_to(piece[None], (outer,) + piece.shape), "dp")
    piece = jnp.sum(pieces, axis=0)
    pieces = exchange(jnp.broadcast_to(piece[None], (inner,) + piece.shape), "dap")
    return pieces.reshape(parts.shape)


def per_device(pair, cotangent, lengths, w_in, gain_in, w_out, gain_out):
    blocks, rows, width, channels = pair.shape
    row_ids = lax.axis_index("dap") * rows + lax.iota(jnp.int32, rows)
    column_ids = lax.iota(jnp.int32, width)
    row_mask = (row_ids[None, :] < lengths[:, None]).astype(jnp.float32)
    column_mask = (column_ids[None, :] < lengths[:, None]).astype(jnp.float32)
    cell_mask = row_mask[:, :, None, None] * column_mask[:, None, :, None]
    saved, out_gate, left, right = project(pair, cell_mask, w_in, gain_in)
    both = jnp.concatenate([channel_major(left), channel_major(right)], axis=0)
    both = lax.all_to_all(both, "dap", split_axis=1, concat_axis=2, tiled=True)
    left_cols, right_cols = both[:blocks], both[blocks:]
    product_cols = jnp.einsum(
        "bcik,bcjk->bcij", left_cols, right_cols, preferred_element_type=jnp.float32
    ).astype(jnp.bfloat16)
    product = channel_minor(
        lax.all_to_all(product_cols, "dap", split_axis=2, concat_axis=1, tiled=True)
    )
    grad_product, grad_gate, w_out_part, gain_out_part = output_backward(
        product, out_gate, cotangent, w_out, gain_out
    )
    grad_cols = lax.all_to_all(
        channel_major(grad_product), "dap", split_axis=1, concat_axis=2, tiled=True
    )
    grad_left_cols = jnp.einsum(
        "bcij,bcjk->bcik", grad_cols, right_cols, preferred_element_type=jnp.float32
    ).astype(jnp.bfloat16)
    grad_right_cols = jnp.einsum(
        "bcij,bcik->bcjk", grad_cols, left_cols, preferred_element_type=jnp.float32
    ).astype(jnp.bfloat16)
    both = jnp.concatenate([grad_left_cols, grad_right_cols], axis=0)
    both = lax.all_to_all(both, "dap", split_axis=2, concat_axis=1, tiled=True)
    grad_left_major, grad_right_major = both[:blocks], both[blocks:]
    grad_left = channel_minor(grad_left_major)
    grad_right = channel_minor(grad_right_major)
    grad_pair, w_in_part, gain_in_part = input_backward(
        grad_left, grad_right, grad_gate, saved, cell_mask, w_in, gain_in
    )
    parts = jnp.concatenate([w_in_part, w_out_part], axis=1)
    totals = summed_everywhere(parts)
    w_in_total, w_out_total = totals[:, : 5 * 128], totals[:, 5 * 128 :]
    gain_in_total = jnp.sum(w_in.astype(jnp.float32) * w_in_total, axis=1) / gain_in
    gain_out_total = jnp.sum(w_out.astype(jnp.float32) * w_out_total, axis=1) / gain_out
    factor = 1.0 / (width * math.sqrt(blocks * lax.axis_size("dp")))
    return (
        grad_pair,
        w_in_total * factor,
        gain_in_total * factor,
        w_out_total * factor,
        gain_out_total * factor,
    )


def solution(mesh):
    in_specs = (P("dp", "dap", None, None), P("dp", "dap", None, None), P("dp"), P(), P(), P(), P())
    out_specs = (P("dp", "dap", None, None), P(), P(), P(), P())
    return jax.shard_map(
        per_device, mesh=mesh, in_specs=in_specs, out_specs=out_specs, check_vma=False
    )
```

```python
import math

import jax
import jax.numpy as jnp
from jax import lax
from jax.experimental import pallas as pl
from jax.experimental.pallas import tpu as pltpu
from jax.sharding import PartitionSpec as P

EPSILON = 1e-05
LANES = 128
SUB = 8
BF16 = jnp.bfloat16
F32 = jnp.float32


def dot(first, second, dims):
    return lax.dot_general(first, second, (dims, ((), ())), preferred_element_type=F32)


NN = ((1,), (0,))
NT = ((1,), (1,))
TN = ((0,), (0,))


def sigmoid(x):
    return 0.5 * jnp.tanh(0.5 * x) + 0.5


def identity(size):
    rows = lax.broadcasted_iota(jnp.int32, (size, size), 0)
    columns = lax.broadcasted_iota(jnp.int32, (size, size), 1)
    return (rows == columns).astype(F32).astype(BF16)


def column(gain_row, size):
    return jnp.transpose(jnp.broadcast_to(gain_row, (size, size)))


def norm_sublanes(x):
    scale = 1.0 / x.shape[0]
    centred = x - jnp.sum(x, axis=0, keepdims=True) * scale
    variance = jnp.sum(centred * centred, axis=0, keepdims=True) * scale
    inverse = lax.rsqrt(variance + EPSILON)
    return centred * inverse, inverse


def row_of_masks(scalars_ref, i, width):
    length = scalars_ref[0]
    columns = lax.broadcasted_iota(jnp.int32, (1, width), 1)
    keep = jnp.logical_and(columns < length, scalars_ref[1] + i < length)
    return keep.astype(F32)


def wide(gain, width):
    return jnp.concatenate([gain] * (width // gain.shape[1]), axis=1)


def project_kernel(scalars_ref, pair_ref, w_ref, gain_ref, send_ref, norm_ref, wt_ref, stage_ref):
    rows, width, channels = pair_ref.shape
    eye = identity(channels)
    gain = wide(column(gain_ref[...], channels), width)
    for n in range(4):
        block = w_ref[:, n * channels : (n + 1) * channels]
        wt_ref[n] = jnp.transpose(block.astype(F32)).astype(BF16)
    for i in range(rows):
        hat, _ = norm_sublanes(dot(eye, pair_ref[i], NT))
        norm = (hat * gain).astype(BF16)
        norm_ref[i] = norm
        mask = row_of_masks(scalars_ref, i, width)
        for side in range(2):
            value = dot(wt_ref[2 * side], norm, NN)
            gate = sigmoid(dot(wt_ref[2 * side + 1], norm, NN))
            value = mask * gate * value
            for half in range(width // LANES):
                stage_ref[side, half, pl.ds(i, channels, stride=rows), :] = value[
                    :, half * LANES : (half + 1) * LANES
                ]
    peers = send_ref.shape[0]
    for side in range(2):
        for half in range(width // LANES):
            send_ref[:, side, half] = (
                stage_ref[side, half].reshape(peers, -1, LANES).astype(BF16)
            )


def regroup(block, group):
    peers, _, lanes = block.shape
    block = block.astype(F32).reshape(peers, group, SUB, lanes)
    return [block[:, c].reshape(peers * SUB, lanes).astype(BF16) for c in range(group)]


def product_kernel(got_ref, send_ref, held_ref, stage_ref):
    peers, _, halves, packed, _ = got_ref.shape
    group = packed // SUB
    for side in range(2):
        for half in range(halves):
            for c, block in enumerate(regroup(got_ref[:, side, half], group)):
                held_ref[side, half, c] = block
    for c in range(group):
        for out in range(halves):
            right_rows = pl.ds(out * LANES, LANES)
            total = dot(held_ref[0, 0, c], held_ref[1, 0, c, right_rows, :], NT)
            for half in range(1, halves):
                total = total + dot(held_ref[0, half, c], held_ref[1, half, c, right_rows, :], NT)
            stage_ref[out, :, c * SUB : (c + 1) * SUB, :] = total.reshape(peers, SUB, LANES)
    for out in range(halves):
        send_ref[:, out] = stage_ref[out].astype(BF16)


def output_ahead_kernel(
    scalars_ref, norm_ref, cotangent_ref, w_ref, w_out_ref, gain_ref,
    upstream_ref, factors_ref, gated_ref, slope_ref, wt_ref,
):
    rows, width, channels = cotangent_ref.shape
    eye = identity(channels)
    gain = wide(column(gain_ref[...], channels), width)
    for n in range(5):
        block = w_ref[:, n * channels : (n + 1) * channels]
        wt_ref[n] = jnp.transpose(block.astype(F32)).astype(BF16)
    w_out = w_out_ref[...]
    for i in range(rows):
        norm = norm_ref[i]
        cotangent = dot(eye, cotangent_ref[i], NT)
        out_gate = sigmoid(dot(wt_ref[4], norm, NN))
        gated = cotangent * out_gate
        slope_ref[i] = gated * (1.0 - out_gate)
        gated = gated.astype(BF16)
        gated_ref[i] = gated
        upstream = dot(w_out, gated, NN) * gain
        upstream = upstream - jnp.sum(upstream, axis=0, keepdims=True) * (1.0 / channels)
        for half in range(width // LANES):
            upstream_ref[half, pl.ds(i, channels, stride=rows), :] = upstream[
                :, half * LANES : (half + 1) * LANES
            ]
        mask = row_of_masks(scalars_ref, i, width)
        for side in range(2):
            value = dot(wt_ref[2 * side], norm, NN)
            gate = sigmoid(dot(wt_ref[2 * side + 1], norm, NN))
            masked = mask * gate
            factors_ref[i, 2 * side] = masked
            factors_ref[i, 2 * side + 1] = masked * value * (1.0 - gate)


def norm_blocks(block):
    product = block.astype(F32).reshape(-1, SUB, block.shape[-1])
    return norm_sublanes(product)


def output_back_kernel(got_ref, upstream_ref, send_ref):
    peers, halves, packed, lanes = got_ref.shape
    for half in range(halves):
        hat, inverse = norm_blocks(got_ref[:, half])
        upstream = upstream_ref[half].reshape(hat.shape)
        second = jnp.sum(upstream * hat, axis=0, keepdims=True) * (1.0 / hat.shape[0])
        grad = inverse * (upstream - hat * second)
        send_ref[:, half] = grad.reshape(peers, packed, lanes).astype(BF16)


def output_weights_kernel(
    got_ref, norm_ref, gated_ref, slope_ref, w_out_ref, gain_ref,
    gate_grad_ref, sums_ref, stage_ref,
):
    halves = got_ref.shape[1]
    rows, channels, _ = norm_ref.shape
    gain = column(gain_ref[...], channels)
    w_out_t = jnp.transpose(w_out_ref[...].astype(F32)).astype(BF16)
    for half in range(halves):
        hat, _ = norm_blocks(got_ref[:, half])
        stage_ref[half] = hat.reshape(-1, LANES)
    w_out_sum = jnp.zeros((channels, channels), F32)
    w_gate_sum = jnp.zeros((channels, channels), F32)
    for i in range(rows):
        for half in range(halves):
            lanes = slice(half * LANES, (half + 1) * LANES)
            hat = stage_ref[half, pl.ds(i, channels, stride=rows), :]
            prod_norm = (hat * gain).astype(BF16)
            update = dot(w_out_t, prod_norm, NN)
            gate_grad = (slope_ref[i, :, lanes] * update).astype(BF16)
            gate_grad_ref[i, :, lanes] = gate_grad
            w_out_sum = w_out_sum + dot(prod_norm, gated_ref[i, :, lanes], NT)
            w_gate_sum = w_gate_sum + dot(norm_ref[i, :, lanes], gate_grad, NT)
    sums_ref[0] = w_gate_sum
    sums_ref[1] = w_out_sum


def operands_back_kernel(got_ref, held_ref, send_ref, stage_ref):
    peers, halves, packed, _ = got_ref.shape
    group = packed // SUB
    blocks = [regroup(got_ref[:, half], group) for half in range(halves)]
    for c in range(group):
        for out in range(halves):
            left = None
            for half in range(halves):
                rows = pl.ds(half * LANES, LANES)
                part = dot(blocks[half][c], held_ref[1, out, c, rows, :], NN)
                left = part if left is None else left + part
            stage_ref[0, out, :, c * SUB : (c + 1) * SUB, :] = left.reshape(peers, SUB, LANES)
            for half in range(halves):
                right = dot(blocks[half][c], held_ref[0, out, c], TN)
                span = peers // halves
                stage_ref[1, out, half * span : (half + 1) * span, c * SUB : (c + 1) * SUB, :] = (
                    right.reshape(span, SUB, LANES)
                )
    for side in range(2):
        for out in range(halves):
            send_ref[:, side, out] = stage_ref[side, out].astype(BF16)


def input_weights_kernel(
    got_ref, factors_ref, norm_ref, sums_ref, parts_ref, pieces_ref, stage_ref
):
    halves = got_ref.shape[2]
    rows, channels, _ = norm_ref.shape
    for side in range(2):
        for half in range(halves):
            stage_ref[side, half] = got_ref[:, side, half].astype(F32).reshape(-1, LANES)
    totals = [jnp.zeros((channels, 2 * channels), F32) for _ in range(2)]
    for i in range(rows):
        for half in range(halves):
            lanes = slice(half * LANES, (half + 1) * LANES)
            norm = norm_ref[i, :, lanes]
            for side in range(2):
                grad = stage_ref[side, half, pl.ds(i, channels, stride=rows), :]
                pieces = jnp.concatenate(
                    [
                        (grad * factors_ref[i, 2 * side, :, lanes]).astype(BF16),
                        (grad * factors_ref[i, 2 * side + 1, :, lanes]).astype(BF16),
                    ],
                    axis=0,
                )
                pieces_ref[i, 2 * side * channels : 2 * (side + 1) * channels, lanes] = pieces
                totals[side] = totals[side] + dot(norm, pieces, NT)
    for side in range(2):
        for n in range(2):
            parts_ref[2 * side + n] = totals[side][:, n * channels : (n + 1) * channels]
    parts_ref[4] = sums_ref[0]
    parts_ref[5] = sums_ref[1]


def input_back_kernel(pieces_ref, gate_grad_ref, pair_ref, w_ref, gain_ref, out_ref):
    rows, width, channels = pair_ref.shape
    eye = identity(channels)
    gain = wide(column(gain_ref[...], channels), width)
    for i in range(rows):
        hat, inverse = norm_sublanes(dot(eye, pair_ref[i], NT))
        grad = dot(w_ref[:, : 4 * channels], pieces_ref[i], NN)
        grad = grad + dot(w_ref[:, 4 * channels :], gate_grad_ref[i], NN)
        grad = grad * gain
        first = jnp.sum(grad, axis=0, keepdims=True) * (1.0 / channels)
        second = jnp.sum(grad * hat, axis=0, keepdims=True) * (1.0 / channels)
        grad = inverse * (grad - first - hat * second)
        out_ref[i] = jnp.transpose(grad).astype(BF16)


def fold_kernel(got_ref, send_ref):
    total = jnp.sum(got_ref[...].astype(F32), axis=0)
    send_ref[...] = jnp.broadcast_to(total[None], send_ref.shape).astype(send_ref.dtype)


def finish_kernel(
    factor, got_ref, w_ref, gain_in_ref, w_out_ref, gain_out_ref,
    w_in_grad_ref, gain_in_grad_ref, w_out_grad_ref, gain_out_grad_ref,
):
    channels = w_out_ref.shape[0]
    dots = jnp.zeros((channels, channels), F32)
    for n in range(5):
        total = got_ref[n] * factor
        lanes = slice(n * channels, (n + 1) * channels)
        w_in_grad_ref[:, lanes] = total
        dots = dots + total * w_ref[:, lanes].astype(F32)
    gain_in_grad_ref[...] = jnp.sum(jnp.transpose(dots), axis=0, keepdims=True) / gain_in_ref[...]
    total = got_ref[5] * factor
    w_out_grad_ref[...] = total
    dots = total * w_out_ref[...].astype(F32)
    gain_out_grad_ref[...] = jnp.sum(jnp.transpose(dots), axis=0, keepdims=True) / gain_out_ref[...]


def exchange(values, axis):
    return lax.all_to_all(values, axis, split_axis=0, concat_axis=0, tiled=True)


def call(kernel, name, out_shape, scratch=(), scalars=False, inputs=1, flops=10**9):
    in_specs = [pl.BlockSpec(memory_space=pltpu.VMEM)] * inputs
    if scalars:
        in_specs[0] = pl.BlockSpec(memory_space=pltpu.SMEM)
    return pl.pallas_call(
        kernel,
        out_shape=[jax.ShapeDtypeStruct(shape, dtype) for shape, dtype in out_shape],
        in_specs=in_specs,
        out_specs=[pl.BlockSpec(memory_space=pltpu.VMEM)] * len(out_shape),
        scratch_shapes=[pltpu.VMEM(shape, dtype) for shape, dtype in scratch],
        compiler_params=pltpu.CompilerParams(vmem_limit_bytes=40 * 2**20),
        cost_estimate=pl.CostEstimate(flops=flops, bytes_accessed=4 * 2**20, transcendentals=0),
        name=name,
    )


def per_device(pair, cotangent, lengths, w_in, gain_in, w_out, gain_out):
    _, rows, width, channels = pair.shape
    inner, outer = lax.axis_size("dap"), lax.axis_size("dp")
    halves, packed = width // LANES, channels // inner * rows
    group = channels // inner
    pair, cotangent = pair[0], cotangent[0]
    gain_in, gain_out = gain_in[None], gain_out[None]
    scalars = jnp.stack([lengths[0], lax.axis_index("dap").astype(jnp.int32) * rows])
    one_side, two_sides = (inner, halves, packed, LANES), (inner, 2, halves, packed, LANES)
    flat = (rows, channels, width)

    send, norm = call(
        project_kernel, "project", [(two_sides, BF16), (flat, BF16)],
        [((4, channels, channels), BF16), ((2, halves, channels * rows, LANES), F32)],
        scalars=True, inputs=4,
    )(scalars, pair, w_in, gain_in)
    got_operands = exchange(send, "dap")
    upstream, factors, gated, slope = call(
        output_ahead_kernel, "output_ahead",
        [
            ((halves, channels * rows, LANES), F32),
            ((rows, 4, channels, width), F32),
            (flat, BF16),
            (flat, F32),
        ],
        [((5, channels, channels), BF16)],
        scalars=True, inputs=6, flops=6 * 10**9,
    )(scalars, norm, cotangent, w_in, w_out, gain_out)

    send, held = call(
        product_kernel, "product",
        [(one_side, BF16), ((2, halves, group, width, LANES), BF16)],
        [((halves, inner, packed, LANES), F32)],
    )(got_operands)
    got_product = exchange(send, "dap")

    (send,) = call(output_back_kernel, "output_back", [(one_side, BF16)], inputs=2)(
        got_product, upstream
    )
    got_grad = exchange(send, "dap")
    gate_grad, sums = call(
        output_weights_kernel, "output_weights",
        [(flat, BF16), ((2, channels, channels), F32)],
        [((halves, channels * rows, LANES), F32)],
        inputs=6, flops=4 * 10**9,
    )(got_product, norm, gated, slope, w_out, gain_out)

    (send,) = call(
        operands_back_kernel, "operands_back", [(two_sides, BF16)],
        [((2, halves, inner, packed, LANES), F32)], inputs=2,
    )(got_grad, held)
    got_operand_grads = exchange(send, "dap")

    parts, pieces = call(
        input_weights_kernel, "input_weights",
        [((6, channels, channels), F32), ((rows, 4 * channels, width), BF16)],
        [((2, halves, channels * rows, LANES), F32)], inputs=4,
    )(got_operand_grads, factors, norm, sums)
    share = 6 * channels // inner
    got = exchange(parts.reshape(inner, share, channels), "dap")
    (pair_grad,) = call(
        input_back_kernel, "input_back", [((rows, width, channels), BF16)], inputs=5,
        flops=6 * 10**9,
    )(pieces, gate_grad, pair, w_in, gain_in)
    (send,) = call(fold_kernel, "fold_inner", [((outer, share, channels), F32)])(got)
    got = exchange(send, "dp")
    (send,) = call(fold_kernel, "fold_outer", [((inner, share, channels), F32)])(got)
    got = exchange(send, "dap").reshape(6, channels, channels)
    factor = 1.0 / (width * math.sqrt(outer))

    def finish(*refs):
        finish_kernel(factor, *refs)

    w_in_grad, gain_in_grad, w_out_grad, gain_out_grad = call(
        finish, "finish",
        [
            ((channels, 5 * channels), F32),
            ((1, channels), F32),
            ((channels, channels), F32),
            ((1, channels), F32),
        ],
        inputs=5,
    )(got, w_in, gain_in, w_out, gain_out)
    return (pair_grad[None], w_in_grad, gain_in_grad[0], w_out_grad, gain_out_grad[0])


def solution(mesh):
    in_specs = (P("dp", "dap", None, None), P("dp", "dap", None, None), P("dp"), P(), P(), P(), P())
    out_specs = (P("dp", "dap", None, None), P(), P(), P(), P())
    return jax.shard_map(
        per_device, mesh=mesh, in_specs=in_specs, out_specs=out_specs, check_vma=False
    )
```

```python
import math

import jax
import jax.numpy as jnp
from jax import lax
from jax.experimental import pallas as pl
from jax.experimental.pallas import tpu as pltpu
from jax.sharding import PartitionSpec as P

EPSILON = 1e-05
LANES = 128
SUB = 8
BF16 = jnp.bfloat16
F32 = jnp.float32


def dot(first, second, dims):
    return lax.dot_general(first, second, (dims, ((), ())), preferred_element_type=F32)


NN = ((1,), (0,))
NT = ((1,), (1,))
TN = ((0,), (0,))


def sigmoid(x):
    return 0.5 * jnp.tanh(0.5 * x) + 0.5


def identity(size):
    rows = lax.broadcasted_iota(jnp.int32, (size, size), 0)
    columns = lax.broadcasted_iota(jnp.int32, (size, size), 1)
    return (rows == columns).astype(F32).astype(BF16)


def column(gain_row, size):
    return jnp.transpose(jnp.broadcast_to(gain_row, (size, size)))


def norm_sublanes(x):
    scale = 1.0 / x.shape[0]
    centred = x - jnp.sum(x, axis=0, keepdims=True) * scale
    variance = jnp.sum(centred * centred, axis=0, keepdims=True) * scale
    inverse = lax.rsqrt(variance + EPSILON)
    return centred * inverse, inverse


def row_of_masks(length, i, rows, width):
    columns = lax.broadcasted_iota(jnp.int32, (1, width), 1)
    row = lax.axis_index("dap").astype(jnp.int32) * rows + i
    return jnp.logical_and(columns < length, row < length).astype(F32)


def wide(gain, width):
    return jnp.concatenate([gain] * (width // gain.shape[1]), axis=1)


def transposed_blocks(w_ref, wt_ref):
    for n in range(wt_ref.shape[0]):
        block = w_ref[:, n * LANES : (n + 1) * LANES]
        wt_ref[n] = jnp.transpose(block.astype(F32)).astype(BF16)


def output_ahead(
    length, norm_ref, cotangent_ref, wt_ref, w_out_ref, gain_ref, outs, stages, sems
):
    rows, width, channels = cotangent_ref.shape
    upstream_ref, factors_ref, gated_ref, slope_ref = stages
    eye = identity(channels)
    gain = wide(column(gain_ref[...], channels), width)
    w_out = w_out_ref[...]
    copies = []
    for i in range(rows):
        norm = norm_ref[i]
        cotangent = dot(eye, cotangent_ref[i], NT)
        out_gate = sigmoid(dot(wt_ref[4], norm, NN))
        gated = cotangent * out_gate
        slope_ref[i] = gated * (1.0 - out_gate)
        gated = gated.astype(BF16)
        gated_ref[i] = gated
        upstream = dot(w_out, gated, NN) * gain
        upstream = upstream - jnp.sum(upstream, axis=0, keepdims=True) * (1.0 / channels)
        for half in range(width // LANES):
            upstream_ref[half, pl.ds(i, channels, stride=rows), :] = upstream[
                :, half * LANES : (half + 1) * LANES
            ]
        mask = row_of_masks(length, i, rows, width)
        for side in range(2):
            value = dot(wt_ref[2 * side], norm, NN)
            gate = sigmoid(dot(wt_ref[2 * side + 1], norm, NN))
            masked = mask * gate
            factors_ref[i, 2 * side] = masked.astype(BF16)
            factors_ref[i, 2 * side + 1] = (masked * value * (1.0 - gate)).astype(BF16)
        for n in range(1, 4):
            copies.append(
                pltpu.make_async_copy(stages[n].at[i], outs[n].at[i], sems.at[n, i])
            )
            copies[-1].start()
    for half in range(width // LANES):
        copies.append(
            pltpu.make_async_copy(upstream_ref.at[half], outs[0].at[half], sems.at[0, half])
        )
        copies[-1].start()
    for copy in copies:
        copy.wait()


def first_core():
    return lax.rem(lax.axis_index("dp").astype(jnp.int32), 2) == 0


def project_kernel(
    lengths_ref, pair_hbm, cotangent_hbm, w_hbm, gain_hbm, w_out_hbm, gain_out_hbm,
    send_ref, norm_ref, *rest,
):
    outs, stages = rest[:4], rest[4:8]
    pair_ref, cotangent_ref, w_ref, gain_ref, w_out_ref, gain_out_ref = rest[8:14]
    wt_ref, stage_ref, sems, in_sems = rest[14:]
    rows, width, channels = pair_ref.shape
    length = lengths_ref[0]
    whole = [
        pltpu.make_async_copy(source, target, in_sems.at[2, n])
        for n, (source, target) in enumerate(
            (
                (w_hbm, w_ref),
                (gain_hbm, gain_ref),
                (w_out_hbm, w_out_ref),
                (gain_out_hbm, gain_out_ref),
            )
        )
    ]
    by_row = [
        [
            pltpu.make_async_copy(source.at[i], target.at[i], in_sems.at[n, i])
            for i in range(rows)
        ]
        for n, (source, target) in enumerate(
            ((pair_hbm, pair_ref), (cotangent_hbm, cotangent_ref))
        )
    ]
    for copy in whole[:2] + by_row[0] + whole[2:] + by_row[1]:
        copy.start()
    eye = identity(channels)
    whole[0].wait()
    transposed_blocks(w_ref, wt_ref)
    whole[1].wait()
    gain = wide(column(gain_ref[...], channels), width)
    for i in range(rows):
        by_row[0][i].wait()
        hat, _ = norm_sublanes(dot(eye, pair_ref[i], NT))
        norm = (hat * gain).astype(BF16)
        norm_ref[i] = norm
        mask = row_of_masks(length, i, rows, width)
        for side in range(2):
            value = dot(wt_ref[2 * side], norm, NN)
            gate = sigmoid(dot(wt_ref[2 * side + 1], norm, NN))
            value = mask * gate * value
            for half in range(width // LANES):
                stage_ref[side, half, pl.ds(i, channels, stride=rows), :] = value[
                    :, half * LANES : (half + 1) * LANES
                ]
    peers = send_ref.shape[0]
    for side in range(2):
        for half in range(width // LANES):
            send_ref[:, side, half] = (
                stage_ref[side, half].reshape(peers, -1, LANES).astype(BF16)
            )
    for copy in whole[2:] + by_row[1]:
        copy.wait()

    @pl.when(first_core())
    def _():
        output_ahead(
            length, norm_ref, cotangent_ref, wt_ref, w_out_ref, gain_out_ref, outs, stages, sems
        )


def output_ahead_kernel(
    lengths_ref, norm_ref, cotangent_ref, w_ref, w_out_ref, gain_ref, *rest
):
    outs, stages = rest[4:8], rest[8:12]
    wt_ref, sems = rest[12:]

    @pl.when(jnp.logical_not(first_core()))
    def _():
        transposed_blocks(w_ref, wt_ref)
        output_ahead(
            lengths_ref[0], norm_ref, cotangent_ref, wt_ref, w_out_ref, gain_ref, outs, stages, sems
        )


def regroup(block, group):
    peers, _, lanes = block.shape
    block = block.astype(F32).reshape(peers, group, SUB, lanes)
    return [block[:, c].reshape(peers * SUB, lanes).astype(BF16) for c in range(group)]


def product_kernel(got_ref, send_ref, held_ref, stage_ref):
    peers, _, halves, packed, _ = got_ref.shape
    group = packed // SUB
    for side in range(2):
        for half in range(halves):
            for c, block in enumerate(regroup(got_ref[:, side, half], group)):
                held_ref[side, half, c] = block
    for c in range(group):
        for out in range(halves):
            right_rows = pl.ds(out * LANES, LANES)
            total = dot(held_ref[0, 0, c], held_ref[1, 0, c, right_rows, :], NT)
            for half in range(1, halves):
                total = total + dot(held_ref[0, half, c], held_ref[1, half, c, right_rows, :], NT)
            stage_ref[out, :, c * SUB : (c + 1) * SUB, :] = total.reshape(peers, SUB, LANES)
    for out in range(halves):
        send_ref[:, out] = stage_ref[out].astype(BF16)


def norm_blocks(block):
    product = block.astype(F32).reshape(-1, SUB, block.shape[-1])
    return norm_sublanes(product)


def output_back_kernel(got_ref, upstream_hbm, send_ref, upstream_ref, sems):
    peers, halves, packed, lanes = got_ref.shape
    copies = [
        pltpu.make_async_copy(upstream_hbm.at[half], upstream_ref.at[half], sems.at[half])
        for half in range(halves)
    ]
    for copy in copies:
        copy.start()
    for half in range(halves):
        hat, inverse = norm_blocks(got_ref[:, half])
        copies[half].wait()
        upstream = upstream_ref[half].reshape(hat.shape)
        second = jnp.sum(upstream * hat, axis=0, keepdims=True) * (1.0 / hat.shape[0])
        grad = inverse * (upstream - hat * second)
        send_ref[:, half] = grad.reshape(peers, packed, lanes).astype(BF16)


def output_weights_kernel(
    got_ref, norm_ref, gated_ref, slope_ref, w_out_ref, gain_ref,
    gate_grad_ref, sums_ref, stage_ref,
):
    halves = got_ref.shape[1]
    rows, channels, _ = norm_ref.shape
    gain = column(gain_ref[...], channels)
    w_out_t = jnp.transpose(w_out_ref[...].astype(F32)).astype(BF16)
    for half in range(halves):
        hat, _ = norm_blocks(got_ref[:, half])
        stage_ref[half] = hat.reshape(-1, LANES)
    w_out_sum = jnp.zeros((channels, channels), F32)
    w_gate_sum = jnp.zeros((channels, channels), F32)
    for i in range(rows):
        for half in range(halves):
            lanes = slice(half * LANES, (half + 1) * LANES)
            hat = stage_ref[half, pl.ds(i, channels, stride=rows), :]
            prod_norm = (hat * gain).astype(BF16)
            update = dot(w_out_t, prod_norm, NN)
            gate_grad = (slope_ref[i, :, lanes] * update).astype(BF16)
            gate_grad_ref[i, :, lanes] = gate_grad
            w_out_sum = w_out_sum + dot(prod_norm, gated_ref[i, :, lanes], NT)
            w_gate_sum = w_gate_sum + dot(norm_ref[i, :, lanes], gate_grad, NT)
    sums_ref[0] = w_gate_sum
    sums_ref[1] = w_out_sum


def operands_back_kernel(got_ref, held_ref, send_ref, stage_ref):
    peers, halves, packed, _ = got_ref.shape
    group = packed // SUB
    blocks = [regroup(got_ref[:, half], group) for half in range(halves)]
    for c in range(group):
        for out in range(halves):
            left = None
            for half in range(halves):
                rows = pl.ds(half * LANES, LANES)
                part = dot(blocks[half][c], held_ref[1, out, c, rows, :], NN)
                left = part if left is None else left + part
            stage_ref[0, out, :, c * SUB : (c + 1) * SUB, :] = left.reshape(peers, SUB, LANES)
            for half in range(halves):
                right = dot(blocks[half][c], held_ref[0, out, c], TN)
                span = peers // halves
                stage_ref[1, out, half * span : (half + 1) * span, c * SUB : (c + 1) * SUB, :] = (
                    right.reshape(span, SUB, LANES)
                )
    for side in range(2):
        for out in range(halves):
            send_ref[:, side, out] = stage_ref[side, out].astype(BF16)


def input_weights_kernel(
    got_ref, factors_hbm, norm_ref, sums_ref, parts_ref, pieces_ref, stage_ref, factors_ref, sems
):
    halves = got_ref.shape[2]
    rows, channels, _ = norm_ref.shape
    copies = [
        pltpu.make_async_copy(factors_hbm.at[i], factors_ref.at[i], sems.at[i])
        for i in range(rows)
    ]
    for copy in copies:
        copy.start()
    for side in range(2):
        for half in range(halves):
            stage_ref[side, half] = got_ref[:, side, half].astype(F32).reshape(-1, LANES)
    totals = [jnp.zeros((channels, 2 * channels), F32) for _ in range(2)]
    for i in range(rows):
        copies[i].wait()
        for half in range(halves):
            lanes = slice(half * LANES, (half + 1) * LANES)
            norm = norm_ref[i, :, lanes]
            for side in range(2):
                grad = stage_ref[side, half, pl.ds(i, channels, stride=rows), :]
                pieces = jnp.concatenate(
                    [
                        (grad * factors_ref[i, 2 * side, :, lanes]).astype(BF16),
                        (grad * factors_ref[i, 2 * side + 1, :, lanes]).astype(BF16),
                    ],
                    axis=0,
                )
                pieces_ref[i, 2 * side * channels : 2 * (side + 1) * channels, lanes] = pieces
                totals[side] = totals[side] + dot(norm, pieces, NT)
    for side in range(2):
        for n in range(2):
            parts_ref[2 * side + n] = totals[side][:, n * channels : (n + 1) * channels].astype(BF16)
    parts_ref[4] = sums_ref[0].astype(BF16)
    parts_ref[5] = sums_ref[1].astype(BF16)


def input_back_kernel(pieces_ref, gate_grad_ref, pair_ref, w_ref, gain_ref, out_ref):
    rows, width, channels = pair_ref.shape
    eye = identity(channels)
    gain = wide(column(gain_ref[...], channels), width)
    for i in range(rows):
        hat, inverse = norm_sublanes(dot(eye, pair_ref[i], NT))
        grad = dot(w_ref[:, : 4 * channels], pieces_ref[i], NN)
        grad = grad + dot(w_ref[:, 4 * channels :], gate_grad_ref[i], NN)
        grad = grad * gain
        first = jnp.sum(grad, axis=0, keepdims=True) * (1.0 / channels)
        second = jnp.sum(grad * hat, axis=0, keepdims=True) * (1.0 / channels)
        grad = inverse * (grad - first - hat * second)
        out_ref[i] = jnp.transpose(grad).astype(BF16)


def fold_kernel(got_ref, send_ref):
    total = jnp.sum(got_ref[...].astype(F32), axis=0)
    send_ref[...] = jnp.broadcast_to(total[None], send_ref.shape).astype(send_ref.dtype)


def finish_kernel(
    factor, got_ref, w_ref, gain_in_ref, w_out_ref, gain_out_ref,
    w_in_grad_ref, gain_in_grad_ref, w_out_grad_ref, gain_out_grad_ref,
):
    channels = w_out_ref.shape[0]
    dots = jnp.zeros((channels, channels), F32)
    for n in range(5):
        total = got_ref[n].astype(F32) * factor
        lanes = slice(n * channels, (n + 1) * channels)
        w_in_grad_ref[:, lanes] = total
        dots = dots + total * w_ref[:, lanes].astype(F32)
    gain_in_grad_ref[...] = jnp.sum(jnp.transpose(dots), axis=0, keepdims=True) / gain_in_ref[...]
    total = got_ref[5].astype(F32) * factor
    w_out_grad_ref[...] = total
    dots = total * w_out_ref[...].astype(F32)
    gain_out_grad_ref[...] = jnp.sum(jnp.transpose(dots), axis=0, keepdims=True) / gain_out_ref[...]


def exchange(values, axis):
    return lax.all_to_all(values, axis, split_axis=0, concat_axis=0, tiled=True)


VMEM = pl.BlockSpec(memory_space=pltpu.VMEM)
SMEM = pl.BlockSpec(memory_space=pltpu.SMEM)
HBM = pl.BlockSpec(memory_space=pltpu.HBM)
COPIES = pltpu.SemaphoreType.DMA


def call(kernel, name, ins, outs, scratch=(), aliases=None, flops=10**9, grant=24):
    return pl.pallas_call(
        kernel,
        out_shape=[jax.ShapeDtypeStruct(shape, dtype) for shape, dtype, _ in outs],
        in_specs=ins,
        out_specs=[spec for _, _, spec in outs],
        scratch_shapes=[pltpu.VMEM(*item) if isinstance(item, tuple) else item for item in scratch],
        input_output_aliases=aliases or {},
        compiler_params=pltpu.CompilerParams(vmem_limit_bytes=grant * 2**20),
        cost_estimate=pl.CostEstimate(flops=flops, bytes_accessed=4 * 2**20, transcendentals=0),
        name=name,
    )


def per_device(pair, cotangent, lengths, w_in, gain_in, w_out, gain_out):
    _, rows, width, channels = pair.shape
    inner, outer = lax.axis_size("dap"), lax.axis_size("dp")
    halves, group = width // LANES, channels // inner
    packed = group * rows
    pair, cotangent = pair[0], cotangent[0]
    gain_in, gain_out = gain_in[None], gain_out[None]
    one_side, two_sides = (inner, halves, packed, LANES), (inner, 2, halves, packed, LANES)
    flat, square, row = (rows, channels, width), (channels, channels), (1, channels)
    mixed = (halves, channels * rows, LANES)

    ahead = [
        (mixed, F32),
        ((rows, 4, channels, width), BF16),
        (flat, BF16),
        (flat, F32),
    ]
    ahead_outs = [(shape, dtype, HBM) for shape, dtype in ahead]
    transposed = ((5,) + square, BF16)
    send, norm, *ahead_parts = call(
        project_kernel, "project", [SMEM] + [HBM] * 6,
        [(two_sides, BF16, VMEM), (flat, BF16, VMEM)] + ahead_outs,
        ahead
        + [
            ((rows, width, channels), BF16),
            ((rows, width, channels), BF16),
            ((channels, 5 * channels), BF16),
            (row, F32),
            (square, BF16),
            (row, F32),
            transposed,
            ((2,) + mixed, F32),
            COPIES((4, rows)),
            COPIES((3, rows)),
        ],
        grant=60,
    )(lengths, pair, cotangent, w_in, gain_in, w_out, gain_out)
    got_operands = exchange(send, "dap")
    upstream, factors, gated, slope = call(
        output_ahead_kernel, "output_ahead", [SMEM] + [VMEM] * 5 + [HBM] * 4, ahead_outs,
        ahead + [transposed, COPIES((4, rows))],
        aliases={6 + n: n for n in range(4)}, flops=6 * 10**9, grant=60,
    )(lengths, norm, cotangent, w_in, w_out, gain_out, *ahead_parts)

    send, held = call(
        product_kernel, "product", [VMEM],
        [(one_side, BF16, VMEM), ((2, halves, group, width, LANES), BF16, VMEM)],
        [((halves, inner, packed, LANES), F32)],
    )(got_operands)
    got_product = exchange(send, "dap")

    (send,) = call(
        output_back_kernel, "output_back", [VMEM, HBM], [(one_side, BF16, VMEM)],
        [(mixed, F32), COPIES((halves,))], grant=60,
    )(got_product, upstream)
    got_grad = exchange(send, "dap")
    gate_grad, sums = call(
        output_weights_kernel, "output_weights", [VMEM] * 6,
        [(flat, BF16, VMEM), ((2,) + square, F32, VMEM)],
        [(mixed, F32)], flops=4 * 10**9,
    )(got_product, norm, gated, slope, w_out, gain_out)

    (send,) = call(
        operands_back_kernel, "operands_back", [VMEM, VMEM], [(two_sides, BF16, VMEM)],
        [((2, halves, inner, packed, LANES), F32)],
    )(got_grad, held)
    got_operand_grads = exchange(send, "dap")

    parts, pieces = call(
        input_weights_kernel, "input_weights", [VMEM, HBM, VMEM, VMEM],
        [((6,) + square, BF16, VMEM), ((rows, 4 * channels, width), BF16, VMEM)],
        [((2,) + mixed, F32), ahead[1], COPIES((rows,))], grant=60,
    )(got_operand_grads, factors, norm, sums)
    share = 6 * channels // inner
    got = exchange(parts.reshape(inner, share, channels), "dap")
    (pair_grad,) = call(
        input_back_kernel, "input_back", [VMEM] * 5, [((rows, width, channels), BF16, VMEM)],
        flops=6 * 10**9,
    )(pieces, gate_grad, pair, w_in, gain_in)
    (send,) = call(
        fold_kernel, "fold_inner", [VMEM], [((outer, share, channels), BF16, VMEM)]
    )(got)
    got = exchange(send, "dp")
    (send,) = call(
        fold_kernel, "fold_outer", [VMEM], [((inner, share, channels), BF16, VMEM)]
    )(got)
    got = exchange(send, "dap").reshape((6,) + square)
    factor = 1.0 / (width * math.sqrt(outer))

    def finish(*refs):
        finish_kernel(factor, *refs)

    w_in_grad, gain_in_grad, w_out_grad, gain_out_grad = call(
        finish, "finish", [VMEM] * 5,
        [
            ((channels, 5 * channels), F32, VMEM),
            (row, F32, VMEM),
            (square, F32, VMEM),
            (row, F32, VMEM),
        ],
    )(got, w_in, gain_in, w_out, gain_out)
    return (pair_grad[None], w_in_grad, gain_in_grad[0], w_out_grad, gain_out_grad[0])


def solution(mesh):
    in_specs = (P("dp", "dap", None, None), P("dp", "dap", None, None), P("dp"), P(), P(), P(), P())
    out_specs = (P("dp", "dap", None, None), P(), P(), P(), P())
    return jax.shard_map(
        per_device, mesh=mesh, in_specs=in_specs, out_specs=out_specs, check_vma=False
    )
```

```python
import math

import jax
import jax.numpy as jnp
from jax import lax
from jax.experimental import pallas as pl
from jax.experimental.pallas import tpu as pltpu
from jax.sharding import PartitionSpec as P

EPSILON = 1e-05
LANES = 128
SUB = 8
BF16 = jnp.bfloat16
F32 = jnp.float32


def dot(first, second, dims):
    return lax.dot_general(first, second, (dims, ((), ())), preferred_element_type=F32)


NN = ((1,), (0,))
NT = ((1,), (1,))
TN = ((0,), (0,))


def sigmoid(x):
    return 0.5 * jnp.tanh(0.5 * x) + 0.5


def identity(size):
    rows = lax.broadcasted_iota(jnp.int32, (size, size), 0)
    columns = lax.broadcasted_iota(jnp.int32, (size, size), 1)
    return (rows == columns).astype(F32).astype(BF16)


def column(gain_row, size):
    return jnp.transpose(jnp.broadcast_to(gain_row, (size, size)))


def norm_sublanes(x):
    scale = 1.0 / x.shape[0]
    centred = x - jnp.sum(x, axis=0, keepdims=True) * scale
    variance = jnp.sum(centred * centred, axis=0, keepdims=True) * scale
    inverse = lax.rsqrt(variance + EPSILON)
    return centred * inverse, inverse


def row_of_masks(length, i, rows, width):
    columns = lax.broadcasted_iota(jnp.int32, (1, width), 1)
    row = lax.axis_index("dap").astype(jnp.int32) * rows + i
    return jnp.logical_and(columns < length, row < length).astype(F32)


def wide(gain, width):
    return jnp.concatenate([gain] * (width // gain.shape[1]), axis=1)


def transposed_blocks(w_ref, wt_ref):
    for n in range(wt_ref.shape[0]):
        block = w_ref[:, n * LANES : (n + 1) * LANES]
        wt_ref[n] = jnp.transpose(block.astype(F32)).astype(BF16)


def output_ahead(
    length, norm_ref, cotangent_ref, wt_ref, w_out_ref, gain_ref, outs, stages, sems
):
    rows, width, channels = cotangent_ref.shape
    upstream_ref, factors_ref, gated_ref, slope_ref = stages
    eye = identity(channels)
    gain = wide(column(gain_ref[...], channels), width)
    w_out = w_out_ref[...]
    copies = []
    for i in range(rows):
        norm = norm_ref[i]
        cotangent = dot(eye, cotangent_ref[i], NT)
        out_gate = sigmoid(dot(wt_ref[4], norm, NN))
        gated = cotangent * out_gate
        slope_ref[i] = gated * (1.0 - out_gate)
        gated = gated.astype(BF16)
        gated_ref[i] = gated
        upstream = dot(w_out, gated, NN) * gain
        upstream = upstream - jnp.sum(upstream, axis=0, keepdims=True) * (1.0 / channels)
        for half in range(width // LANES):
            upstream_ref[half, pl.ds(i, channels, stride=rows), :] = upstream[
                :, half * LANES : (half + 1) * LANES
            ]
        mask = row_of_masks(length, i, rows, width)
        for side in range(2):
            value = dot(wt_ref[2 * side], norm, NN)
            gate = sigmoid(dot(wt_ref[2 * side + 1], norm, NN))
            masked = mask * gate
            factors_ref[i, 2 * side] = masked.astype(BF16)
            factors_ref[i, 2 * side + 1] = (masked * value * (1.0 - gate)).astype(BF16)
        for n in range(1, 4):
            copies.append(
                pltpu.make_async_copy(stages[n].at[i], outs[n].at[i], sems.at[n, i])
            )
            copies[-1].start()
    for half in range(width // LANES):
        copies.append(
            pltpu.make_async_copy(upstream_ref.at[half], outs[0].at[half], sems.at[0, half])
        )
        copies[-1].start()
    for copy in copies:
        copy.wait()


def first_core():
    return lax.rem(lax.axis_index("dp").astype(jnp.int32), 2) == 0


def project_kernel(
    lengths_ref, pair_hbm, cotangent_hbm, w_hbm, gain_hbm, w_out_hbm, gain_out_hbm,
    send_hbm, norm_hbm, *rest,
):
    outs, stages = rest[:4], rest[4:8]
    pair_ref, cotangent_ref, w_ref, gain_ref, w_out_ref, gain_out_ref = rest[8:14]
    wt_ref, stage_ref, send_ref, norm_ref, sems, in_sems = rest[14:]
    rows, width, channels = pair_ref.shape
    length = lengths_ref[0]
    whole = [
        pltpu.make_async_copy(source, target, in_sems.at[2, n])
        for n, (source, target) in enumerate(
            (
                (w_hbm, w_ref),
                (gain_hbm, gain_ref),
                (w_out_hbm, w_out_ref),
                (gain_out_hbm, gain_out_ref),
            )
        )
    ]
    by_row = [
        [
            pltpu.make_async_copy(source.at[i], target.at[i], in_sems.at[n, i])
            for i in range(rows)
        ]
        for n, (source, target) in enumerate(
            ((pair_hbm, pair_ref), (cotangent_hbm, cotangent_ref))
        )
    ]
    for copy in whole[:2] + by_row[0] + whole[2:] + by_row[1]:
        copy.start()
    eye = identity(channels)
    whole[0].wait()
    transposed_blocks(w_ref, wt_ref)
    whole[1].wait()
    gain = wide(column(gain_ref[...], channels), width)
    done = []
    for i in range(rows):
        by_row[0][i].wait()
        hat, _ = norm_sublanes(dot(eye, pair_ref[i], NT))
        norm = (hat * gain).astype(BF16)
        norm_ref[i] = norm
        done.append(pltpu.make_async_copy(norm_ref.at[i], norm_hbm.at[i], in_sems.at[3, i]))
        done[-1].start()
        mask = row_of_masks(length, i, rows, width)
        for side in range(2):
            value = dot(wt_ref[2 * side], norm, NN)
            gate = sigmoid(dot(wt_ref[2 * side + 1], norm, NN))
            value = mask * gate * value
            for half in range(width // LANES):
                stage_ref[side, half, pl.ds(i, channels, stride=rows), :] = value[
                    :, half * LANES : (half + 1) * LANES
                ]
    peers = send_ref.shape[0]
    for side in range(2):
        for half in range(width // LANES):
            send_ref[:, side, half] = (
                stage_ref[side, half].reshape(peers, -1, LANES).astype(BF16)
            )
            done.append(
                pltpu.make_async_copy(
                    send_ref.at[:, side, half],
                    send_hbm.at[:, side, half],
                    in_sems.at[2, 4 + 2 * side + half],
                )
            )
            done[-1].start()
    for copy in whole[2:] + by_row[1]:
        copy.wait()

    @pl.when(first_core())
    def _():
        output_ahead(
            length, norm_ref, cotangent_ref, wt_ref, w_out_ref, gain_out_ref, outs, stages, sems
        )

    for copy in done:
        copy.wait()


def output_ahead_kernel(
    lengths_ref, norm_ref, cotangent_ref, w_ref, w_out_ref, gain_ref, *rest
):
    outs, stages = rest[4:8], rest[8:12]
    wt_ref, sems = rest[12:]

    @pl.when(jnp.logical_not(first_core()))
    def _():
        transposed_blocks(w_ref, wt_ref)
        output_ahead(
            lengths_ref[0], norm_ref, cotangent_ref, wt_ref, w_out_ref, gain_ref, outs, stages, sems
        )


def regroup(block, group):
    peers, _, lanes = block.shape
    block = block.astype(F32).reshape(peers, group, SUB, lanes)
    return [block[:, c].reshape(peers * SUB, lanes).astype(BF16) for c in range(group)]


def product_kernel(got_ref, send_ref, held_ref, stage_ref):
    peers, _, halves, packed, _ = got_ref.shape
    group = packed // SUB
    for side in range(2):
        for half in range(halves):
            for c, block in enumerate(regroup(got_ref[:, side, half], group)):
                held_ref[side, half, c] = block
    for c in range(group):
        for out in range(halves):
            right_rows = pl.ds(out * LANES, LANES)
            total = dot(held_ref[0, 0, c], held_ref[1, 0, c, right_rows, :], NT)
            for half in range(1, halves):
                total = total + dot(held_ref[0, half, c], held_ref[1, half, c, right_rows, :], NT)
            stage_ref[out, :, c * SUB : (c + 1) * SUB, :] = total.reshape(peers, SUB, LANES)
    for out in range(halves):
        send_ref[:, out] = stage_ref[out].astype(BF16)


def norm_blocks(block):
    product = block.astype(F32).reshape(-1, SUB, block.shape[-1])
    return norm_sublanes(product)


def output_back_kernel(got_ref, upstream_ref, send_ref):
    peers, halves, packed, lanes = got_ref.shape
    for half in range(halves):
        hat, inverse = norm_blocks(got_ref[:, half])
        upstream = upstream_ref[half].reshape(hat.shape)
        second = jnp.sum(upstream * hat, axis=0, keepdims=True) * (1.0 / hat.shape[0])
        grad = inverse * (upstream - hat * second)
        send_ref[:, half] = grad.reshape(peers, packed, lanes).astype(BF16)


def output_weights_kernel(
    got_ref, norm_ref, gated_ref, slope_ref, w_out_ref, gain_ref,
    gate_grad_ref, sums_ref, stage_ref,
):
    halves = got_ref.shape[1]
    rows, channels, _ = norm_ref.shape
    gain = column(gain_ref[...], channels)
    w_out_t = jnp.transpose(w_out_ref[...].astype(F32)).astype(BF16)
    for half in range(halves):
        hat, _ = norm_blocks(got_ref[:, half])
        stage_ref[half] = hat.reshape(-1, LANES)
    w_out_sum = jnp.zeros((channels, channels), F32)
    w_gate_sum = jnp.zeros((channels, channels), F32)
    for i in range(rows):
        for half in range(halves):
            lanes = slice(half * LANES, (half + 1) * LANES)
            hat = stage_ref[half, pl.ds(i, channels, stride=rows), :]
            prod_norm = (hat * gain).astype(BF16)
            update = dot(w_out_t, prod_norm, NN)
            gate_grad = (slope_ref[i, :, lanes] * update).astype(BF16)
            gate_grad_ref[i, :, lanes] = gate_grad
            w_out_sum = w_out_sum + dot(prod_norm, gated_ref[i, :, lanes], NT)
            w_gate_sum = w_gate_sum + dot(norm_ref[i, :, lanes], gate_grad, NT)
    sums_ref[0] = w_gate_sum
    sums_ref[1] = w_out_sum


def operands_back_kernel(got_ref, held_ref, send_ref, stage_ref):
    peers, halves, packed, _ = got_ref.shape
    group = packed // SUB
    blocks = [regroup(got_ref[:, half], group) for half in range(halves)]
    for c in range(group):
        for out in range(halves):
            left = None
            for half in range(halves):
                rows = pl.ds(half * LANES, LANES)
                part = dot(blocks[half][c], held_ref[1, out, c, rows, :], NN)
                left = part if left is None else left + part
            stage_ref[0, out, :, c * SUB : (c + 1) * SUB, :] = left.reshape(peers, SUB, LANES)
            for half in range(halves):
                right = dot(blocks[half][c], held_ref[0, out, c], TN)
                span = peers // halves
                stage_ref[1, out, half * span : (half + 1) * span, c * SUB : (c + 1) * SUB, :] = (
                    right.reshape(span, SUB, LANES)
                )
    for side in range(2):
        for out in range(halves):
            send_ref[:, side, out] = stage_ref[side, out].astype(BF16)


def unpack(got_ref, stage_ref):
    for side in range(got_ref.shape[1]):
        for half in range(got_ref.shape[2]):
            stage_ref[side, half] = got_ref[:, side, half].astype(F32).reshape(-1, LANES)


def pieces_of(stage_ref, factors_ref, i, side, half, rows, channels):
    lanes = slice(half * LANES, (half + 1) * LANES)
    grad = stage_ref[side, half, pl.ds(i, channels, stride=rows), :]
    return jnp.concatenate(
        [
            (grad * factors_ref[i, 2 * side + n, :, lanes].astype(F32)).astype(BF16)
            for n in range(2)
        ],
        axis=0,
    )


def input_weights_kernel(got_ref, factors_ref, norm_ref, sums_ref, parts_ref, stage_ref):
    halves = got_ref.shape[2]
    rows, channels, _ = norm_ref.shape
    unpack(got_ref, stage_ref)
    totals = [jnp.zeros((channels, 2 * channels), F32) for _ in range(2)]
    for i in range(rows):
        for half in range(halves):
            norm = norm_ref[i, :, half * LANES : (half + 1) * LANES]
            for side in range(2):
                pieces = pieces_of(stage_ref, factors_ref, i, side, half, rows, channels)
                totals[side] = totals[side] + dot(norm, pieces, NT)
    for side in range(2):
        for n in range(2):
            parts_ref[2 * side + n] = totals[side][:, n * channels : (n + 1) * channels].astype(BF16)
    parts_ref[4] = sums_ref[0].astype(BF16)
    parts_ref[5] = sums_ref[1].astype(BF16)


def input_back_kernel(
    got_ref, factors_ref, gate_grad_ref, pair_ref, w_ref, gain_ref, out_ref, stage_ref
):
    rows, width, channels = pair_ref.shape
    eye = identity(channels)
    gain = wide(column(gain_ref[...], channels), width)
    unpack(got_ref, stage_ref)
    for i in range(rows):
        hat, inverse = norm_sublanes(dot(eye, pair_ref[i], NT))
        grad = dot(w_ref[:, 4 * channels :], gate_grad_ref[i], NN)
        for side in range(2):
            pieces = jnp.concatenate(
                [
                    pieces_of(stage_ref, factors_ref, i, side, half, rows, channels)
                    for half in range(width // LANES)
                ],
                axis=1,
            )
            block = w_ref[:, 2 * side * channels : 2 * (side + 1) * channels]
            grad = grad + dot(block, pieces, NN)
        grad = grad * gain
        first = jnp.sum(grad, axis=0, keepdims=True) * (1.0 / channels)
        second = jnp.sum(grad * hat, axis=0, keepdims=True) * (1.0 / channels)
        grad = inverse * (grad - first - hat * second)
        out_ref[i] = jnp.transpose(grad).astype(BF16)


def fold_kernel(got_ref, send_ref):
    total = jnp.sum(got_ref[...].astype(F32), axis=0)
    send_ref[...] = jnp.broadcast_to(total[None], send_ref.shape).astype(send_ref.dtype)


def finish_kernel(
    factor, got_ref, w_ref, gain_in_ref, w_out_ref, gain_out_ref,
    w_in_grad_ref, gain_in_grad_ref, w_out_grad_ref, gain_out_grad_ref,
):
    channels = w_out_ref.shape[0]
    dots = jnp.zeros((channels, channels), F32)
    for n in range(5):
        total = got_ref[n].astype(F32) * factor
        lanes = slice(n * channels, (n + 1) * channels)
        w_in_grad_ref[:, lanes] = total
        dots = dots + total * w_ref[:, lanes].astype(F32)
    gain_in_grad_ref[...] = jnp.sum(jnp.transpose(dots), axis=0, keepdims=True) / gain_in_ref[...]
    total = got_ref[5].astype(F32) * factor
    w_out_grad_ref[...] = total
    dots = total * w_out_ref[...].astype(F32)
    gain_out_grad_ref[...] = jnp.sum(jnp.transpose(dots), axis=0, keepdims=True) / gain_out_ref[...]


def exchange(values, axis):
    return lax.all_to_all(values, axis, split_axis=0, concat_axis=0, tiled=True)


VMEM = pl.BlockSpec(memory_space=pltpu.VMEM)
SMEM = pl.BlockSpec(memory_space=pltpu.SMEM)
HBM = pl.BlockSpec(memory_space=pltpu.HBM)
COPIES = pltpu.SemaphoreType.DMA


def call(kernel, name, ins, outs, scratch=(), aliases=None, flops=10**9, grant=24):
    return pl.pallas_call(
        kernel,
        out_shape=[jax.ShapeDtypeStruct(shape, dtype) for shape, dtype, _ in outs],
        in_specs=ins,
        out_specs=[spec for _, _, spec in outs],
        scratch_shapes=[pltpu.VMEM(*item) if isinstance(item, tuple) else item for item in scratch],
        input_output_aliases=aliases or {},
        compiler_params=pltpu.CompilerParams(vmem_limit_bytes=grant * 2**20),
        cost_estimate=pl.CostEstimate(flops=flops, bytes_accessed=4 * 2**20, transcendentals=0),
        name=name,
    )


def per_device(pair, cotangent, lengths, w_in, gain_in, w_out, gain_out):
    _, rows, width, channels = pair.shape
    inner, outer = lax.axis_size("dap"), lax.axis_size("dp")
    halves, group = width // LANES, channels // inner
    packed = group * rows
    pair, cotangent = pair[0], cotangent[0]
    gain_in, gain_out = gain_in[None], gain_out[None]
    one_side, two_sides = (inner, halves, packed, LANES), (inner, 2, halves, packed, LANES)
    flat, square, row = (rows, channels, width), (channels, channels), (1, channels)
    mixed = (halves, channels * rows, LANES)

    ahead = [
        (mixed, F32),
        ((rows, 4, channels, width), BF16),
        (flat, BF16),
        (flat, F32),
    ]
    ahead_outs = [(shape, dtype, HBM) for shape, dtype in ahead]
    transposed = ((5,) + square, BF16)
    send, norm, *ahead_parts = call(
        project_kernel, "project", [SMEM] + [HBM] * 6,
        [(two_sides, BF16, HBM), (flat, BF16, HBM)] + ahead_outs,
        ahead
        + [
            ((rows, width, channels), BF16),
            ((rows, width, channels), BF16),
            ((channels, 5 * channels), BF16),
            (row, F32),
            (square, BF16),
            (row, F32),
            transposed,
            ((2,) + mixed, F32),
            (two_sides, BF16),
            (flat, BF16),
            COPIES((4, rows)),
            COPIES((4, rows)),
        ],
        grant=60,
    )(lengths, pair, cotangent, w_in, gain_in, w_out, gain_out)
    got_operands = exchange(send, "dap")
    upstream, factors, gated, slope = call(
        output_ahead_kernel, "output_ahead", [SMEM] + [VMEM] * 5 + [HBM] * 4, ahead_outs,
        ahead + [transposed, COPIES((4, rows))],
        aliases={6 + n: n for n in range(4)}, flops=6 * 10**9, grant=60,
    )(lengths, norm, cotangent, w_in, w_out, gain_out, *ahead_parts)

    got_operands, upstream = lax.optimization_barrier((got_operands, upstream))
    send, held = call(
        product_kernel, "product", [VMEM],
        [(one_side, BF16, VMEM), ((2, halves, group, width, LANES), BF16, VMEM)],
        [((halves, inner, packed, LANES), F32)],
    )(got_operands)
    got_product = exchange(send, "dap")

    (send,) = call(
        output_back_kernel, "output_back", [VMEM, VMEM], [(one_side, BF16, VMEM)],
    )(got_product, upstream)
    got_grad = exchange(send, "dap")
    gate_grad, sums = call(
        output_weights_kernel, "output_weights", [VMEM] * 6,
        [(flat, BF16, VMEM), ((2,) + square, F32, VMEM)],
        [(mixed, F32)], flops=4 * 10**9,
    )(got_product, norm, gated, slope, w_out, gain_out)

    (send,) = call(
        operands_back_kernel, "operands_back", [VMEM, VMEM], [(two_sides, BF16, VMEM)],
        [((2, halves, inner, packed, LANES), F32)],
    )(got_grad, held)
    got_operand_grads = exchange(send, "dap")

    (parts,) = call(
        input_weights_kernel, "input_weights", [VMEM] * 4, [((6,) + square, BF16, VMEM)],
        [((2,) + mixed, F32)],
    )(got_operand_grads, factors, norm, sums)
    share = 6 * channels // inner
    got = exchange(parts.reshape(inner, share, channels), "dap")
    (pair_grad,) = call(
        input_back_kernel, "input_back", [VMEM] * 6, [((rows, width, channels), BF16, VMEM)],
        [((2,) + mixed, F32)], flops=6 * 10**9,
    )(got_operand_grads, factors, gate_grad, pair, w_in, gain_in)
    (send,) = call(
        fold_kernel, "fold_inner", [VMEM], [((outer, share, channels), BF16, VMEM)]
    )(got)
    got = exchange(send, "dp")
    (send,) = call(
        fold_kernel, "fold_outer", [VMEM], [((inner, share, channels), BF16, VMEM)]
    )(got)
    got = exchange(send, "dap").reshape((6,) + square)
    factor = 1.0 / (width * math.sqrt(outer))

    def finish(*refs):
        finish_kernel(factor, *refs)

    w_in_grad, gain_in_grad, w_out_grad, gain_out_grad = call(
        finish, "finish", [VMEM] * 5,
        [
            ((channels, 5 * channels), F32, VMEM),
            (row, F32, VMEM),
            (square, F32, VMEM),
            (row, F32, VMEM),
        ],
    )(got, w_in, gain_in, w_out, gain_out)
    return (pair_grad[None], w_in_grad, gain_in_grad[0], w_out_grad, gain_out_grad[0])


def solution(mesh):
    in_specs = (P("dp", "dap", None, None), P("dp", "dap", None, None), P("dp"), P(), P(), P(), P())
    out_specs = (P("dp", "dap", None, None), P(), P(), P(), P())
    return jax.shard_map(
        per_device, mesh=mesh, in_specs=in_specs, out_specs=out_specs, check_vma=False
    )
```

```python
import math

import jax
import jax.numpy as jnp
from jax import lax
from jax.experimental import pallas as pl
from jax.experimental.pallas import tpu as pltpu
from jax.sharding import PartitionSpec as P

EPSILON = 1e-05
LANES = 128
SUB = 8
BF16 = jnp.bfloat16
F32 = jnp.float32


def dot(first, second, dims):
    return lax.dot_general(first, second, (dims, ((), ())), preferred_element_type=F32)


NN = ((1,), (0,))
NT = ((1,), (1,))
TN = ((0,), (0,))


def sigmoid(x):
    return 0.5 * jnp.tanh(0.5 * x) + 0.5


def identity(size):
    rows = lax.broadcasted_iota(jnp.int32, (size, size), 0)
    columns = lax.broadcasted_iota(jnp.int32, (size, size), 1)
    return (rows == columns).astype(F32).astype(BF16)


def column(gain_row, size):
    return jnp.transpose(jnp.broadcast_to(gain_row, (size, size)))


def norm_sublanes(x):
    scale = 1.0 / x.shape[0]
    centred = x - jnp.sum(x, axis=0, keepdims=True) * scale
    variance = jnp.sum(centred * centred, axis=0, keepdims=True) * scale
    inverse = lax.rsqrt(variance + EPSILON)
    return centred * inverse, inverse


def row_of_masks(length, i, rows, width):
    columns = lax.broadcasted_iota(jnp.int32, (1, width), 1)
    row = lax.axis_index("dap").astype(jnp.int32) * rows + i
    return jnp.logical_and(columns < length, row < length).astype(F32)


def wide(gain, width):
    return jnp.concatenate([gain] * (width // gain.shape[1]), axis=1)


def transposed_blocks(w_ref, wt_ref):
    eye = identity(LANES)
    for n in range(wt_ref.shape[0] // LANES):
        rows = slice(n * LANES, (n + 1) * LANES)
        wt_ref[rows] = dot(eye, w_ref[:, rows], NT).astype(BF16)


def projections(wt_ref, norm, blocks):
    channels = norm.shape[0]
    whole = dot(wt_ref[: blocks * channels], norm, NN)
    return [whole[n * channels : (n + 1) * channels] for n in range(blocks)]


def output_ahead(
    length, norm_ref, cotangent_ref, wt_ref, w_out_ref, gain_ref, outs, stages, sems
):
    rows, width, channels = cotangent_ref.shape
    upstream_ref, factors_ref, gated_ref, slope_ref = stages
    eye = identity(channels)
    gain = wide(column(gain_ref[...], channels), width)
    w_out = w_out_ref[...]
    copies = []
    for i in range(rows):
        norm = norm_ref[i]
        cotangent = dot(eye, cotangent_ref[i], NT)
        projected = projections(wt_ref, norm, 5)
        out_gate = sigmoid(projected[4])
        gated = cotangent * out_gate
        slope_ref[i] = gated * (1.0 - out_gate)
        gated = gated.astype(BF16)
        gated_ref[i] = gated
        upstream = dot(w_out, gated, NN) * gain
        upstream = upstream - jnp.sum(upstream, axis=0, keepdims=True) * (1.0 / channels)
        for half in range(width // LANES):
            upstream_ref[half, pl.ds(i, channels, stride=rows), :] = upstream[
                :, half * LANES : (half + 1) * LANES
            ]
        mask = row_of_masks(length, i, rows, width)
        for side in range(2):
            value, gate = projected[2 * side], sigmoid(projected[2 * side + 1])
            masked = mask * gate
            factors_ref[i, 2 * side] = masked.astype(BF16)
            factors_ref[i, 2 * side + 1] = (masked * value * (1.0 - gate)).astype(BF16)
        if 2 * (i + 1) % rows == 0:
            some = pl.ds(i + 1 - rows // 2, rows // 2)
            copies.append(
                pltpu.make_async_copy(factors_ref.at[some], outs[1].at[some], sems.at[1, i])
            )
            copies[-1].start()
    for n in (0, 2, 3):
        copies.append(pltpu.make_async_copy(stages[n], outs[n], sems.at[n, 0]))
        copies[-1].start()
    for copy in copies:
        copy.wait()


def first_core():
    return lax.rem(lax.axis_index("dp").astype(jnp.int32), 2) == 0


def project_kernel(
    lengths_ref, pair_hbm, cotangent_hbm, w_hbm, gain_hbm, w_out_hbm, gain_out_hbm,
    send_hbm, norm_hbm, *rest,
):
    outs, stages = rest[:4], rest[4:8]
    pair_ref, cotangent_ref, w_ref, gain_ref, w_out_ref, gain_out_ref = rest[8:14]
    wt_ref, stage_ref, send_ref, norm_ref, sems, in_sems = rest[14:]
    rows, width, channels = pair_ref.shape
    length = lengths_ref[0]
    def fetch(source, target, n):
        return pltpu.make_async_copy(source, target, in_sems.at[n])

    first = [
        fetch(w_hbm, w_ref, 0),
        fetch(gain_hbm, gain_ref, 1),
        fetch(pair_hbm.at[: rows // 2], pair_ref.at[: rows // 2], 2),
        fetch(pair_hbm.at[rows // 2 :], pair_ref.at[rows // 2 :], 3),
    ]
    later = [
        fetch(cotangent_hbm, cotangent_ref, 4),
        fetch(w_out_hbm, w_out_ref, 5),
        fetch(gain_out_hbm, gain_out_ref, 6),
    ]
    for copy in first:
        copy.start()

    @pl.when(first_core())
    def _():
        for copy in later:
            copy.start()

    eye = identity(channels)
    first[0].wait()
    transposed_blocks(w_ref, wt_ref)
    first[1].wait()
    gain = wide(column(gain_ref[...], channels), width)
    for i in range(rows):
        if 2 * i % rows == 0:
            first[2 + 2 * i // rows].wait()
        hat, _ = norm_sublanes(dot(eye, pair_ref[i], NT))
        norm = (hat * gain).astype(BF16)
        norm_ref[i] = norm
        projected = projections(wt_ref, norm, 4)
        mask = row_of_masks(length, i, rows, width)
        for side in range(2):
            value, gate = projected[2 * side], sigmoid(projected[2 * side + 1])
            value = mask * gate * value
            for half in range(width // LANES):
                stage_ref[side, half, pl.ds(i, channels, stride=rows), :] = value[
                    :, half * LANES : (half + 1) * LANES
                ]
    done = [fetch(norm_ref, norm_hbm, 7)]
    done[0].start()
    peers = send_ref.shape[0]
    for side in range(2):
        for half in range(width // LANES):
            send_ref[:, side, half] = (
                stage_ref[side, half].reshape(peers, -1, LANES).astype(BF16)
            )
        done.append(fetch(send_ref.at[:, side], send_hbm.at[:, side], 8 + side))
        done[-1].start()

    @pl.when(first_core())
    def _():
        for copy in later:
            copy.wait()
        output_ahead(
            length, norm_ref, cotangent_ref, wt_ref, w_out_ref, gain_out_ref, outs, stages, sems
        )

    for copy in done:
        copy.wait()


def output_ahead_kernel(
    lengths_ref, norm_ref, cotangent_ref, w_ref, w_out_ref, gain_ref, *rest
):
    outs, stages = rest[4:8], rest[8:12]
    wt_ref, sems = rest[12:]

    @pl.when(jnp.logical_not(first_core()))
    def _():
        transposed_blocks(w_ref, wt_ref)
        output_ahead(
            lengths_ref[0], norm_ref, cotangent_ref, wt_ref, w_out_ref, gain_ref, outs, stages, sems
        )


def regroup(block, group):
    peers, _, lanes = block.shape
    block = block.astype(F32).reshape(peers, group, SUB, lanes)
    return [block[:, c].reshape(peers * SUB, lanes).astype(BF16) for c in range(group)]


def product_kernel(got_ref, send_ref, held_ref, stage_ref):
    peers, _, halves, packed, _ = got_ref.shape
    group = packed // SUB
    for side in range(2):
        for half in range(halves):
            for c, block in enumerate(regroup(got_ref[:, side, half], group)):
                held_ref[side, half, c] = block
    for c in range(group):
        for out in range(halves):
            right_rows = pl.ds(out * LANES, LANES)
            total = dot(held_ref[0, 0, c], held_ref[1, 0, c, right_rows, :], NT)
            for half in range(1, halves):
                total = total + dot(held_ref[0, half, c], held_ref[1, half, c, right_rows, :], NT)
            stage_ref[out, :, c * SUB : (c + 1) * SUB, :] = total.reshape(peers, SUB, LANES)
    for out in range(halves):
        send_ref[:, out] = stage_ref[out].astype(BF16)


def norm_blocks(block):
    product = block.astype(F32).reshape(-1, SUB, block.shape[-1])
    return norm_sublanes(product)


def output_back_kernel(got_ref, upstream_ref, send_ref):
    peers, halves, packed, lanes = got_ref.shape
    for half in range(halves):
        hat, inverse = norm_blocks(got_ref[:, half])
        upstream = upstream_ref[half].reshape(hat.shape)
        second = jnp.sum(upstream * hat, axis=0, keepdims=True) * (1.0 / hat.shape[0])
        grad = inverse * (upstream - hat * second)
        send_ref[:, half] = grad.reshape(peers, packed, lanes).astype(BF16)


def output_weights_kernel(
    got_ref, norm_ref, gated_ref, slope_ref, w_out_ref, gain_ref,
    gate_grad_ref, sums_ref, stage_ref,
):
    halves = got_ref.shape[1]
    rows, channels, _ = norm_ref.shape
    gain = column(gain_ref[...], channels)
    w_out_t = jnp.transpose(w_out_ref[...].astype(F32)).astype(BF16)
    for half in range(halves):
        hat, _ = norm_blocks(got_ref[:, half])
        stage_ref[half] = hat.reshape(-1, LANES)
    w_out_sum = jnp.zeros((channels, channels), F32)
    w_gate_sum = jnp.zeros((channels, channels), F32)
    for i in range(rows):
        for half in range(halves):
            lanes = slice(half * LANES, (half + 1) * LANES)
            hat = stage_ref[half, pl.ds(i, channels, stride=rows), :]
            prod_norm = (hat * gain).astype(BF16)
            update = dot(w_out_t, prod_norm, NN)
            gate_grad = (slope_ref[i, :, lanes] * update).astype(BF16)
            gate_grad_ref[i, :, lanes] = gate_grad
            w_out_sum = w_out_sum + dot(prod_norm, gated_ref[i, :, lanes], NT)
            w_gate_sum = w_gate_sum + dot(norm_ref[i, :, lanes], gate_grad, NT)
    sums_ref[0] = w_gate_sum
    sums_ref[1] = w_out_sum


def operands_back_kernel(got_ref, held_ref, send_ref, stage_ref):
    peers, halves, packed, _ = got_ref.shape
    group = packed // SUB
    blocks = [regroup(got_ref[:, half], group) for half in range(halves)]
    for c in range(group):
        for out in range(halves):
            left = None
            for half in range(halves):
                rows = pl.ds(half * LANES, LANES)
                part = dot(blocks[half][c], held_ref[1, out, c, rows, :], NN)
                left = part if left is None else left + part
            stage_ref[0, out, :, c * SUB : (c + 1) * SUB, :] = left.reshape(peers, SUB, LANES)
            for half in range(halves):
                right = dot(blocks[half][c], held_ref[0, out, c], TN)
                span = peers // halves
                stage_ref[1, out, half * span : (half + 1) * span, c * SUB : (c + 1) * SUB, :] = (
                    right.reshape(span, SUB, LANES)
                )
    for side in range(2):
        for out in range(halves):
            send_ref[:, side, out] = stage_ref[side, out].astype(BF16)


def unpack(got_ref, stage_ref):
    for side in range(got_ref.shape[1]):
        for half in range(got_ref.shape[2]):
            stage_ref[side, half] = got_ref[:, side, half].astype(F32).reshape(-1, LANES)


def pieces_of(stage_ref, factors_ref, i, side, half, rows, channels):
    lanes = slice(half * LANES, (half + 1) * LANES)
    grad = stage_ref[side, half, pl.ds(i, channels, stride=rows), :]
    return jnp.concatenate(
        [
            (grad * factors_ref[i, 2 * side + n, :, lanes].astype(F32)).astype(BF16)
            for n in range(2)
        ],
        axis=0,
    )


def input_weights_kernel(got_ref, factors_ref, norm_ref, sums_ref, parts_ref, stage_ref):
    halves = got_ref.shape[2]
    rows, channels, _ = norm_ref.shape
    unpack(got_ref, stage_ref)
    totals = [jnp.zeros((channels, 2 * channels), F32) for _ in range(2)]
    for i in range(rows):
        for half in range(halves):
            norm = norm_ref[i, :, half * LANES : (half + 1) * LANES]
            for side in range(2):
                pieces = pieces_of(stage_ref, factors_ref, i, side, half, rows, channels)
                totals[side] = totals[side] + dot(norm, pieces, NT)
    for side in range(2):
        for n in range(2):
            parts_ref[2 * side + n] = totals[side][:, n * channels : (n + 1) * channels].astype(BF16)
    parts_ref[4] = sums_ref[0].astype(BF16)
    parts_ref[5] = sums_ref[1].astype(BF16)


def input_back_kernel(
    got_ref, factors_ref, gate_grad_ref, pair_ref, w_ref, gain_ref, out_ref, stage_ref
):
    rows, width, channels = pair_ref.shape
    eye = identity(channels)
    gain = wide(column(gain_ref[...], channels), width)
    unpack(got_ref, stage_ref)
    for i in range(rows):
        hat, inverse = norm_sublanes(dot(eye, pair_ref[i], NT))
        grad = dot(w_ref[:, 4 * channels :], gate_grad_ref[i], NN)
        for side in range(2):
            pieces = jnp.concatenate(
                [
                    pieces_of(stage_ref, factors_ref, i, side, half, rows, channels)
                    for half in range(width // LANES)
                ],
                axis=1,
            )
            block = w_ref[:, 2 * side * channels : 2 * (side + 1) * channels]
            grad = grad + dot(block, pieces, NN)
        grad = grad * gain
        first = jnp.sum(grad, axis=0, keepdims=True) * (1.0 / channels)
        second = jnp.sum(grad * hat, axis=0, keepdims=True) * (1.0 / channels)
        grad = inverse * (grad - first - hat * second)
        out_ref[i] = jnp.transpose(grad).astype(BF16)


def fold_kernel(got_ref, send_ref):
    total = jnp.sum(got_ref[...].astype(F32), axis=0)
    send_ref[...] = jnp.broadcast_to(total[None], send_ref.shape).astype(send_ref.dtype)


def finish_kernel(
    factor, got_ref, w_ref, gain_in_ref, w_out_ref, gain_out_ref,
    w_in_grad_ref, gain_in_grad_ref, w_out_grad_ref, gain_out_grad_ref,
):
    channels = w_out_ref.shape[0]
    dots = jnp.zeros((channels, channels), F32)
    for n in range(5):
        total = got_ref[n].astype(F32) * factor
        lanes = slice(n * channels, (n + 1) * channels)
        w_in_grad_ref[:, lanes] = total
        dots = dots + total * w_ref[:, lanes].astype(F32)
    gain_in_grad_ref[...] = jnp.sum(jnp.transpose(dots), axis=0, keepdims=True) / gain_in_ref[...]
    total = got_ref[5].astype(F32) * factor
    w_out_grad_ref[...] = total
    dots = total * w_out_ref[...].astype(F32)
    gain_out_grad_ref[...] = jnp.sum(jnp.transpose(dots), axis=0, keepdims=True) / gain_out_ref[...]


def exchange(values, axis):
    return lax.all_to_all(values, axis, split_axis=0, concat_axis=0, tiled=True)


VMEM = pl.BlockSpec(memory_space=pltpu.VMEM)
SMEM = pl.BlockSpec(memory_space=pltpu.SMEM)
HBM = pl.BlockSpec(memory_space=pltpu.HBM)
COPIES = pltpu.SemaphoreType.DMA


def call(kernel, name, ins, outs, scratch=(), aliases=None, flops=10**9, grant=24):
    return pl.pallas_call(
        kernel,
        out_shape=[jax.ShapeDtypeStruct(shape, dtype) for shape, dtype, _ in outs],
        in_specs=ins,
        out_specs=[spec for _, _, spec in outs],
        scratch_shapes=[pltpu.VMEM(*item) if isinstance(item, tuple) else item for item in scratch],
        input_output_aliases=aliases or {},
        compiler_params=pltpu.CompilerParams(vmem_limit_bytes=grant * 2**20),
        cost_estimate=pl.CostEstimate(flops=flops, bytes_accessed=4 * 2**20, transcendentals=0),
        name=name,
    )


def per_device(pair, cotangent, lengths, w_in, gain_in, w_out, gain_out):
    _, rows, width, channels = pair.shape
    inner, outer = lax.axis_size("dap"), lax.axis_size("dp")
    halves, group = width // LANES, channels // inner
    packed = group * rows
    pair, cotangent = pair[0], cotangent[0]
    gain_in, gain_out = gain_in[None], gain_out[None]
    one_side, two_sides = (inner, halves, packed, LANES), (inner, 2, halves, packed, LANES)
    flat, square, row = (rows, channels, width), (channels, channels), (1, channels)
    mixed = (halves, channels * rows, LANES)

    ahead = [
        (mixed, F32),
        ((rows, 4, channels, width), BF16),
        (flat, BF16),
        (flat, F32),
    ]
    ahead_outs = [(shape, dtype, HBM) for shape, dtype in ahead]
    transposed = ((5 * channels, channels), BF16)
    send, norm, *ahead_parts = call(
        project_kernel, "project", [SMEM] + [HBM] * 6,
        [(two_sides, BF16, HBM), (flat, BF16, HBM)] + ahead_outs,
        ahead
        + [
            ((rows, width, channels), BF16),
            ((rows, width, channels), BF16),
            ((channels, 5 * channels), BF16),
            (row, F32),
            (square, BF16),
            (row, F32),
            transposed,
            ((2,) + mixed, F32),
            (two_sides, BF16),
            (flat, BF16),
            COPIES((4, rows)),
            COPIES((10,)),
        ],
        grant=60,
    )(lengths, pair, cotangent, w_in, gain_in, w_out, gain_out)
    got_operands = exchange(send, "dap")
    upstream, factors, gated, slope = call(
        output_ahead_kernel, "output_ahead", [SMEM] + [VMEM] * 5 + [HBM] * 4, ahead_outs,
        ahead + [transposed, COPIES((4, rows))],
        aliases={6 + n: n for n in range(4)}, flops=6 * 10**9, grant=60,
    )(lengths, norm, cotangent, w_in, w_out, gain_out, *ahead_parts)

    got_operands, upstream = lax.optimization_barrier((got_operands, upstream))
    send, held = call(
        product_kernel, "product", [VMEM],
        [(one_side, BF16, VMEM), ((2, halves, group, width, LANES), BF16, VMEM)],
        [((halves, inner, packed, LANES), F32)],
    )(got_operands)
    got_product = exchange(send, "dap")

    (send,) = call(
        output_back_kernel, "output_back", [VMEM, VMEM], [(one_side, BF16, VMEM)],
    )(got_product, upstream)
    got_grad = exchange(send, "dap")
    gate_grad, sums = call(
        output_weights_kernel, "output_weights", [VMEM] * 6,
        [(flat, BF16, VMEM), ((2,) + square, F32, VMEM)],
        [(mixed, F32)], flops=4 * 10**9,
    )(got_product, norm, gated, slope, w_out, gain_out)

    (send,) = call(
        operands_back_kernel, "operands_back", [VMEM, VMEM], [(two_sides, BF16, VMEM)],
        [((2, halves, inner, packed, LANES), F32)],
    )(got_grad, held)
    got_operand_grads = exchange(send, "dap")

    (parts,) = call(
        input_weights_kernel, "input_weights", [VMEM] * 4, [((6,) + square, BF16, VMEM)],
        [((2,) + mixed, F32)],
    )(got_operand_grads, factors, norm, sums)
    share = 6 * channels // inner
    got = exchange(parts.reshape(inner, share, channels), "dap")
    (pair_grad,) = call(
        input_back_kernel, "input_back", [VMEM] * 6, [((rows, width, channels), BF16, VMEM)],
        [((2,) + mixed, F32)], flops=6 * 10**9,
    )(got_operand_grads, factors, gate_grad, pair, w_in, gain_in)
    (send,) = call(
        fold_kernel, "fold_inner", [VMEM], [((outer, share, channels), BF16, VMEM)]
    )(got)
    got = exchange(send, "dp")
    (send,) = call(
        fold_kernel, "fold_outer", [VMEM], [((inner, share, channels), BF16, VMEM)]
    )(got)
    got = exchange(send, "dap").reshape((6,) + square)
    factor = 1.0 / (width * math.sqrt(outer))

    def finish(*refs):
        finish_kernel(factor, *refs)

    w_in_grad, gain_in_grad, w_out_grad, gain_out_grad = call(
        finish, "finish", [VMEM] * 5,
        [
            ((channels, 5 * channels), F32, VMEM),
            (row, F32, VMEM),
            (square, F32, VMEM),
            (row, F32, VMEM),
        ],
    )(got, w_in, gain_in, w_out, gain_out)
    return (pair_grad[None], w_in_grad, gain_in_grad[0], w_out_grad, gain_out_grad[0])


def solution(mesh):
    in_specs = (P("dp", "dap", None, None), P("dp", "dap", None, None), P("dp"), P(), P(), P(), P())
    out_specs = (P("dp", "dap", None, None), P(), P(), P(), P())
    return jax.shard_map(
        per_device, mesh=mesh, in_specs=in_specs, out_specs=out_specs, check_vma=False
    )
```

```python
import math

import jax
import jax.numpy as jnp
from jax import lax
from jax.experimental import pallas as pl
from jax.experimental.pallas import tpu as pltpu
from jax.sharding import PartitionSpec as P

EPSILON = 1e-05
LANES = 128
SUB = 8
BF16 = jnp.bfloat16
F32 = jnp.float32


def dot(first, second, dims):
    return lax.dot_general(first, second, (dims, ((), ())), preferred_element_type=F32)


NN = ((1,), (0,))
NT = ((1,), (1,))
TN = ((0,), (0,))


def sigmoid(x):
    return 0.5 * jnp.tanh(0.5 * x) + 0.5


def identity(size):
    rows = lax.broadcasted_iota(jnp.int32, (size, size), 0)
    columns = lax.broadcasted_iota(jnp.int32, (size, size), 1)
    return (rows == columns).astype(F32).astype(BF16)


def column(gain_row, size):
    return jnp.transpose(jnp.broadcast_to(gain_row, (size, size)))


def norm_sublanes(x):
    scale = 1.0 / x.shape[0]
    centred = x - jnp.sum(x, axis=0, keepdims=True) * scale
    variance = jnp.sum(centred * centred, axis=0, keepdims=True) * scale
    inverse = lax.rsqrt(variance + EPSILON)
    return centred * inverse, inverse


def row_of_masks(length, i, rows, width):
    columns = lax.broadcasted_iota(jnp.int32, (1, width), 1)
    row = lax.axis_index("dap").astype(jnp.int32) * rows + i
    return jnp.logical_and(columns < length, row < length).astype(F32)


def wide(gain, width):
    return jnp.concatenate([gain] * (width // gain.shape[1]), axis=1)


def transposed_blocks(w_ref, wt_ref):
    eye = identity(LANES)
    for n in range(wt_ref.shape[0] // LANES):
        rows = slice(n * LANES, (n + 1) * LANES)
        wt_ref[rows] = dot(eye, w_ref[:, rows], NT).astype(BF16)


def projections(wt_ref, norm, blocks):
    channels = norm.shape[0]
    whole = dot(wt_ref[: blocks * channels], norm, NN)
    return [whole[n * channels : (n + 1) * channels] for n in range(blocks)]


def output_ahead(
    length, norm_ref, cotangent_ref, wt_ref, w_out_ref, gain_ref, outs, stages, sems
):
    rows, width, channels = cotangent_ref.shape
    upstream_ref, factors_ref, gated_ref, slope_ref = stages
    eye = identity(channels)
    gain = wide(column(gain_ref[...], channels), width)
    w_out = w_out_ref[...]
    copies = []
    for i in range(rows):
        norm = norm_ref[i]
        cotangent = jnp.transpose(cotangent_ref[i].astype(F32))
        projected = projections(wt_ref, norm, 5)
        out_gate = sigmoid(projected[4])
        gated = cotangent * out_gate
        slope_ref[i] = gated * (1.0 - out_gate)
        gated = gated.astype(BF16)
        gated_ref[i] = gated
        upstream = dot(w_out, gated, NN) * gain
        upstream = upstream - jnp.sum(upstream, axis=0, keepdims=True) * (1.0 / channels)
        for half in range(width // LANES):
            upstream_ref[half, pl.ds(i, channels, stride=rows), :] = upstream[
                :, half * LANES : (half + 1) * LANES
            ]
        mask = row_of_masks(length, i, rows, width)
        for side in range(2):
            value, gate = projected[2 * side], sigmoid(projected[2 * side + 1])
            masked = mask * gate
            factors_ref[i, 2 * side] = masked.astype(BF16)
            factors_ref[i, 2 * side + 1] = (masked * value * (1.0 - gate)).astype(BF16)
        if 2 * (i + 1) % rows == 0:
            some = pl.ds(i + 1 - rows // 2, rows // 2)
            copies.append(
                pltpu.make_async_copy(factors_ref.at[some], outs[1].at[some], sems.at[1, i])
            )
            copies[-1].start()
    for n in (0, 2, 3):
        copies.append(pltpu.make_async_copy(stages[n], outs[n], sems.at[n, 0]))
        copies[-1].start()
    for copy in copies:
        copy.wait()


def first_core():
    return lax.rem(lax.axis_index("dp").astype(jnp.int32), 2) == 0


def project_kernel(
    lengths_ref, pair_hbm, cotangent_hbm, w_hbm, gain_hbm, w_out_hbm, gain_out_hbm,
    send_hbm, norm_hbm, *rest,
):
    outs, stages = rest[:4], rest[4:8]
    pair_ref, cotangent_ref, w_ref, gain_ref, w_out_ref, gain_out_ref = rest[8:14]
    wt_ref, stage_ref, send_ref, norm_ref, sems, in_sems = rest[14:]
    rows, width, channels = pair_ref.shape
    length = lengths_ref[0]
    def fetch(source, target, n):
        return pltpu.make_async_copy(source, target, in_sems.at[n])

    first = [
        fetch(w_hbm, w_ref, 0),
        fetch(gain_hbm, gain_ref, 1),
        fetch(pair_hbm.at[: rows // 2], pair_ref.at[: rows // 2], 2),
        fetch(pair_hbm.at[rows // 2 :], pair_ref.at[rows // 2 :], 3),
    ]
    later = [
        fetch(cotangent_hbm, cotangent_ref, 4),
        fetch(w_out_hbm, w_out_ref, 5),
        fetch(gain_out_hbm, gain_out_ref, 6),
    ]
    for copy in first:
        copy.start()

    @pl.when(first_core())
    def _():
        for copy in later:
            copy.start()

    eye = identity(channels)
    first[0].wait()
    transposed_blocks(w_ref, wt_ref)
    first[1].wait()
    gain = wide(column(gain_ref[...], channels), width)
    peers = send_ref.shape[0]
    done = []
    for side in range(2):
        for i in range(rows):
            if side == 0:
                if 2 * i % rows == 0:
                    first[2 + 2 * i // rows].wait()
                hat, _ = norm_sublanes(jnp.transpose(pair_ref[i].astype(F32)))
                norm = (hat * gain).astype(BF16)
                norm_ref[i] = norm
            else:
                norm = norm_ref[i]
            blocks = slice(2 * side * channels, 2 * (side + 1) * channels)
            projected = dot(wt_ref[blocks], norm, NN)
            mask = row_of_masks(length, i, rows, width)
            value = mask * sigmoid(projected[channels:]) * projected[:channels]
            for half in range(width // LANES):
                stage_ref[side, half, pl.ds(i, channels, stride=rows), :] = value[
                    :, half * LANES : (half + 1) * LANES
                ]
        for half in range(width // LANES):
            send_ref[:, side, half] = (
                stage_ref[side, half].reshape(peers, -1, LANES).astype(BF16)
            )
        done.append(fetch(send_ref.at[:, side], send_hbm.at[:, side], 8 + side))
        done[-1].start()
        if side == 0:
            done.append(fetch(norm_ref, norm_hbm, 7))
            done[-1].start()

    @pl.when(first_core())
    def _():
        for copy in later:
            copy.wait()
        output_ahead(
            length, norm_ref, cotangent_ref, wt_ref, w_out_ref, gain_out_ref, outs, stages, sems
        )

    for copy in done:
        copy.wait()


def output_ahead_kernel(
    lengths_ref, norm_ref, cotangent_ref, w_ref, w_out_ref, gain_ref, *rest
):
    outs, stages = rest[4:8], rest[8:12]
    wt_ref, sems = rest[12:]

    @pl.when(jnp.logical_not(first_core()))
    def _():
        transposed_blocks(w_ref, wt_ref)
        output_ahead(
            lengths_ref[0], norm_ref, cotangent_ref, wt_ref, w_out_ref, gain_ref, outs, stages, sems
        )


def regroup(block, group):
    peers, _, lanes = block.shape
    block = block.astype(F32).reshape(peers, group, SUB, lanes)
    return [block[:, c].reshape(peers * SUB, lanes).astype(BF16) for c in range(group)]


def product_kernel(got_ref, send_ref, held_ref, stage_ref):
    peers, _, halves, packed, _ = got_ref.shape
    group = packed // SUB
    for side in range(2):
        for half in range(halves):
            for c, block in enumerate(regroup(got_ref[:, side, half], group)):
                held_ref[side, c, :, half * LANES : (half + 1) * LANES] = block
    for c in range(group):
        total = dot(held_ref[0, c], held_ref[1, c], NT)
        for out in range(halves):
            stage_ref[out, :, c * SUB : (c + 1) * SUB, :] = total[
                :, out * LANES : (out + 1) * LANES
            ].reshape(peers, SUB, LANES)
    for out in range(halves):
        send_ref[:, out] = stage_ref[out].astype(BF16)


def norm_blocks(block):
    product = block.astype(F32).reshape(-1, SUB, block.shape[-1])
    return norm_sublanes(product)


def output_back_kernel(got_ref, upstream_ref, send_ref):
    peers, halves, packed, lanes = got_ref.shape
    for half in range(halves):
        hat, inverse = norm_blocks(got_ref[:, half])
        upstream = upstream_ref[half].reshape(hat.shape)
        second = jnp.sum(upstream * hat, axis=0, keepdims=True) * (1.0 / hat.shape[0])
        grad = inverse * (upstream - hat * second)
        send_ref[:, half] = grad.reshape(peers, packed, lanes).astype(BF16)


def output_weights_kernel(
    got_ref, norm_ref, gated_ref, slope_ref, w_out_ref, gain_ref,
    gate_grad_ref, sums_ref, stage_ref,
):
    halves = got_ref.shape[1]
    rows, channels, _ = norm_ref.shape
    gain = column(gain_ref[...], channels)
    w_out_t = jnp.transpose(w_out_ref[...].astype(F32)).astype(BF16)
    for half in range(halves):
        hat, _ = norm_blocks(got_ref[:, half])
        stage_ref[half] = hat.reshape(-1, LANES)
    w_out_sum = jnp.zeros((channels, channels), F32)
    w_gate_sum = jnp.zeros((channels, channels), F32)
    for i in range(rows):
        for half in range(halves):
            lanes = slice(half * LANES, (half + 1) * LANES)
            hat = stage_ref[half, pl.ds(i, channels, stride=rows), :]
            prod_norm = (hat * gain).astype(BF16)
            update = dot(w_out_t, prod_norm, NN)
            gate_grad = (slope_ref[i, :, lanes] * update).astype(BF16)
            gate_grad_ref[i, :, lanes] = gate_grad
            w_out_sum = w_out_sum + dot(prod_norm, gated_ref[i, :, lanes], NT)
            w_gate_sum = w_gate_sum + dot(norm_ref[i, :, lanes], gate_grad, NT)
    sums_ref[0] = w_gate_sum
    sums_ref[1] = w_out_sum


def operands_back_kernel(got_ref, held_ref, send_hbm, stage_ref, send_ref, sems):
    peers, halves, packed, _ = got_ref.shape
    group = packed // SUB
    blocks = [regroup(got_ref[:, half], group) for half in range(halves)]
    grads = [jnp.concatenate([block[c] for block in blocks], axis=1) for c in range(group)]
    copies = []
    for side in (1, 0):
        for c in range(group):
            total = dot(grads[c], held_ref[1 - side, c], TN if side else NN)
            for out in range(halves):
                stage_ref[side, out, :, c * SUB : (c + 1) * SUB, :] = total[
                    :, out * LANES : (out + 1) * LANES
                ].reshape(peers, SUB, LANES)
        for out in range(halves):
            send_ref[:, side, out] = stage_ref[side, out].astype(BF16)
            copies.append(
                pltpu.make_async_copy(
                    send_ref.at[:, side, out], send_hbm.at[:, side, out], sems.at[side, out]
                )
            )
            copies[-1].start()
    for copy in copies:
        copy.wait()


def unpack(got_ref, stage_ref):
    for side in range(got_ref.shape[1]):
        for half in range(got_ref.shape[2]):
            stage_ref[side, half] = got_ref[:, side, half].astype(F32).reshape(-1, LANES)


def pieces_of(stage_ref, factors_ref, i, side, half, rows, channels):
    lanes = slice(half * LANES, (half + 1) * LANES)
    grad = stage_ref[side, half, pl.ds(i, channels, stride=rows), :]
    return jnp.concatenate(
        [
            (grad * factors_ref[i, 2 * side + n, :, lanes].astype(F32)).astype(BF16)
            for n in range(2)
        ],
        axis=0,
    )


def input_weights_kernel(got_ref, factors_ref, norm_ref, sums_ref, parts_ref, stage_ref):
    halves = got_ref.shape[2]
    rows, channels, _ = norm_ref.shape
    unpack(got_ref, stage_ref)
    totals = [jnp.zeros((channels, 2 * channels), F32) for _ in range(2)]
    for i in range(rows):
        for half in range(halves):
            norm = norm_ref[i, :, half * LANES : (half + 1) * LANES]
            for side in range(2):
                pieces = pieces_of(stage_ref, factors_ref, i, side, half, rows, channels)
                totals[side] = totals[side] + dot(norm, pieces, NT)
    for side in range(2):
        for n in range(2):
            parts_ref[2 * side + n] = totals[side][:, n * channels : (n + 1) * channels].astype(BF16)
    parts_ref[4] = sums_ref[0].astype(BF16)
    parts_ref[5] = sums_ref[1].astype(BF16)


def input_back_kernel(
    got_ref, factors_ref, gate_grad_ref, pair_ref, w_ref, gain_ref, out_ref, stage_ref
):
    rows, width, channels = pair_ref.shape
    eye = identity(channels)
    gain = wide(column(gain_ref[...], channels), width)
    unpack(got_ref, stage_ref)
    for i in range(rows):
        hat, inverse = norm_sublanes(jnp.transpose(pair_ref[i].astype(F32)))
        grad = dot(w_ref[:, 4 * channels :], gate_grad_ref[i], NN)
        for side in range(2):
            pieces = jnp.concatenate(
                [
                    pieces_of(stage_ref, factors_ref, i, side, half, rows, channels)
                    for half in range(width // LANES)
                ],
                axis=1,
            )
            block = w_ref[:, 2 * side * channels : 2 * (side + 1) * channels]
            grad = grad + dot(block, pieces, NN)
        grad = grad * gain
        first = jnp.sum(grad, axis=0, keepdims=True) * (1.0 / channels)
        second = jnp.sum(grad * hat, axis=0, keepdims=True) * (1.0 / channels)
        grad = inverse * (grad - first - hat * second)
        out_ref[i] = jnp.transpose(grad).astype(BF16)


def fold_kernel(got_ref, send_ref):
    total = jnp.sum(got_ref[...].astype(F32), axis=0)
    send_ref[...] = jnp.broadcast_to(total[None], send_ref.shape).astype(send_ref.dtype)


def finish_kernel(
    factor, got_ref, w_ref, gain_in_ref, w_out_ref, gain_out_ref,
    w_in_grad_ref, gain_in_grad_ref, w_out_grad_ref, gain_out_grad_ref,
):
    channels = w_out_ref.shape[0]
    dots = jnp.zeros((channels, channels), F32)
    for n in range(5):
        total = got_ref[n].astype(F32) * factor
        lanes = slice(n * channels, (n + 1) * channels)
        w_in_grad_ref[:, lanes] = total
        dots = dots + total * w_ref[:, lanes].astype(F32)
    gain_in_grad_ref[...] = jnp.sum(jnp.transpose(dots), axis=0, keepdims=True) / gain_in_ref[...]
    total = got_ref[5].astype(F32) * factor
    w_out_grad_ref[...] = total
    dots = total * w_out_ref[...].astype(F32)
    gain_out_grad_ref[...] = jnp.sum(jnp.transpose(dots), axis=0, keepdims=True) / gain_out_ref[...]


def exchange(values, axis):
    return lax.all_to_all(values, axis, split_axis=0, concat_axis=0, tiled=True)


VMEM = pl.BlockSpec(memory_space=pltpu.VMEM)
SMEM = pl.BlockSpec(memory_space=pltpu.SMEM)
HBM = pl.BlockSpec(memory_space=pltpu.HBM)
COPIES = pltpu.SemaphoreType.DMA


def call(kernel, name, ins, outs, scratch=(), aliases=None, flops=10**9, grant=24):
    return pl.pallas_call(
        kernel,
        out_shape=[jax.ShapeDtypeStruct(shape, dtype) for shape, dtype, _ in outs],
        in_specs=ins,
        out_specs=[spec for _, _, spec in outs],
        scratch_shapes=[pltpu.VMEM(*item) if isinstance(item, tuple) else item for item in scratch],
        input_output_aliases=aliases or {},
        compiler_params=pltpu.CompilerParams(vmem_limit_bytes=grant * 2**20),
        cost_estimate=pl.CostEstimate(flops=flops, bytes_accessed=4 * 2**20, transcendentals=0),
        name=name,
    )


def per_device(pair, cotangent, lengths, w_in, gain_in, w_out, gain_out):
    _, rows, width, channels = pair.shape
    inner, outer = lax.axis_size("dap"), lax.axis_size("dp")
    halves, group = width // LANES, channels // inner
    packed = group * rows
    pair, cotangent = pair[0], cotangent[0]
    gain_in, gain_out = gain_in[None], gain_out[None]
    one_side, two_sides = (inner, halves, packed, LANES), (inner, 2, halves, packed, LANES)
    flat, square, row = (rows, channels, width), (channels, channels), (1, channels)
    mixed = (halves, channels * rows, LANES)

    ahead = [
        (mixed, F32),
        ((rows, 4, channels, width), BF16),
        (flat, BF16),
        (flat, F32),
    ]
    ahead_outs = [(shape, dtype, HBM) for shape, dtype in ahead]
    transposed = ((5 * channels, channels), BF16)
    send, norm, *ahead_parts = call(
        project_kernel, "project", [SMEM] + [HBM] * 6,
        [(two_sides, BF16, HBM), (flat, BF16, HBM)] + ahead_outs,
        ahead
        + [
            ((rows, width, channels), BF16),
            ((rows, width, channels), BF16),
            ((channels, 5 * channels), BF16),
            (row, F32),
            (square, BF16),
            (row, F32),
            transposed,
            ((2,) + mixed, F32),
            (two_sides, BF16),
            (flat, BF16),
            COPIES((4, rows)),
            COPIES((10,)),
        ],
        grant=60,
    )(lengths, pair, cotangent, w_in, gain_in, w_out, gain_out)
    got_operands = exchange(send, "dap")
    upstream, factors, gated, slope = call(
        output_ahead_kernel, "output_ahead", [SMEM] + [VMEM] * 5 + [HBM] * 4, ahead_outs,
        ahead + [transposed, COPIES((4, rows))],
        aliases={6 + n: n for n in range(4)}, flops=6 * 10**9, grant=60,
    )(lengths, norm, cotangent, w_in, w_out, gain_out, *ahead_parts)

    got_operands, upstream = lax.optimization_barrier((got_operands, upstream))
    send, held = call(
        product_kernel, "product", [VMEM],
        [(one_side, BF16, VMEM), ((2, group, width, width), BF16, VMEM)],
        [((halves, inner, packed, LANES), F32)],
    )(got_operands)
    got_product = exchange(send, "dap")

    (send,) = call(
        output_back_kernel, "output_back", [VMEM, VMEM], [(one_side, BF16, VMEM)],
    )(got_product, upstream)
    got_grad = exchange(send, "dap")
    gate_grad, sums = call(
        output_weights_kernel, "output_weights", [VMEM] * 6,
        [(flat, BF16, VMEM), ((2,) + square, F32, VMEM)],
        [(mixed, F32)], flops=4 * 10**9,
    )(got_product, norm, gated, slope, w_out, gain_out)

    (send,) = call(
        operands_back_kernel, "operands_back", [VMEM, VMEM], [(two_sides, BF16, HBM)],
        [((2, halves, inner, packed, LANES), F32), (two_sides, BF16), COPIES((2, halves))],
    )(got_grad, held)
    got_operand_grads = exchange(send, "dap")

    (parts,) = call(
        input_weights_kernel, "input_weights", [VMEM] * 4, [((6,) + square, BF16, VMEM)],
        [((2,) + mixed, F32)],
    )(got_operand_grads, factors, norm, sums)
    share = 6 * channels // inner
    got = exchange(parts.reshape(inner, share, channels), "dap")
    (pair_grad,) = call(
        input_back_kernel, "input_back", [VMEM] * 6, [((rows, width, channels), BF16, VMEM)],
        [((2,) + mixed, F32)], flops=6 * 10**9,
    )(got_operand_grads, factors, gate_grad, pair, w_in, gain_in)
    (send,) = call(
        fold_kernel, "fold_inner", [VMEM], [((outer, share, channels), BF16, VMEM)]
    )(got)
    got = exchange(send, "dp")
    (send,) = call(
        fold_kernel, "fold_outer", [VMEM], [((inner, share, channels), BF16, VMEM)]
    )(got)
    got = exchange(send, "dap").reshape((6,) + square)
    factor = 1.0 / (width * math.sqrt(outer))

    def finish(*refs):
        finish_kernel(factor, *refs)

    w_in_grad, gain_in_grad, w_out_grad, gain_out_grad = call(
        finish, "finish", [VMEM] * 5,
        [
            ((channels, 5 * channels), F32, VMEM),
            (row, F32, VMEM),
            (square, F32, VMEM),
            (row, F32, VMEM),
        ],
    )(got, w_in, gain_in, w_out, gain_out)
    return (pair_grad[None], w_in_grad, gain_in_grad[0], w_out_grad, gain_out_grad[0])


def solution(mesh):
    in_specs = (P("dp", "dap", None, None), P("dp", "dap", None, None), P("dp"), P(), P(), P(), P())
    out_specs = (P("dp", "dap", None, None), P(), P(), P(), P())
    return jax.shard_map(
        per_device, mesh=mesh, in_specs=in_specs, out_specs=out_specs, check_vma=False
    )
```

```python
import math

import jax
import jax.numpy as jnp
from jax import lax
from jax.experimental import pallas as pl
from jax.experimental.pallas import tpu as pltpu
from jax.sharding import PartitionSpec as P

EPSILON = 1e-05
LANES = 128
SUB = 8
BF16 = jnp.bfloat16
F32 = jnp.float32


def dot(first, second, dims):
    return lax.dot_general(first, second, (dims, ((), ())), preferred_element_type=F32)


NN = ((1,), (0,))
NT = ((1,), (1,))
TN = ((0,), (0,))


def sigmoid(x):
    return 0.5 * jnp.tanh(0.5 * x) + 0.5


def identity(size):
    rows = lax.broadcasted_iota(jnp.int32, (size, size), 0)
    columns = lax.broadcasted_iota(jnp.int32, (size, size), 1)
    return (rows == columns).astype(F32).astype(BF16)


def column(gain_row, size):
    return jnp.transpose(jnp.broadcast_to(gain_row, (size, size)))


def norm_sublanes(x):
    scale = 1.0 / x.shape[0]
    centred = x - jnp.sum(x, axis=0, keepdims=True) * scale
    variance = jnp.sum(centred * centred, axis=0, keepdims=True) * scale
    inverse = lax.rsqrt(variance + EPSILON)
    return centred * inverse, inverse


def row_of_masks(length, i, rows, width):
    columns = lax.broadcasted_iota(jnp.int32, (1, width), 1)
    row = lax.axis_index("dap").astype(jnp.int32) * rows + i
    return jnp.logical_and(columns < length, row < length).astype(F32)


def wide(gain, width):
    return jnp.concatenate([gain] * (width // gain.shape[1]), axis=1)


def transposed_blocks(w_ref, wt_ref):
    eye = identity(LANES)
    for n in range(wt_ref.shape[0] // LANES):
        rows = slice(n * LANES, (n + 1) * LANES)
        wt_ref[rows] = dot(eye, w_ref[:, rows], NT).astype(BF16)


def projections(wt_ref, norm, blocks):
    channels = norm.shape[0]
    whole = dot(wt_ref[: blocks * channels], norm, NN)
    return [whole[n * channels : (n + 1) * channels] for n in range(blocks)]


def output_ahead(
    length, norm_ref, cotangent_ref, wt_ref, w_out_ref, gain_ref, outs, stages, sems
):
    rows, width, channels = cotangent_ref.shape
    upstream_ref, left_ref, gated_ref, slope_ref, right_ref = stages
    factors = (left_ref, right_ref)
    eye = identity(channels)
    gain = wide(column(gain_ref[...], channels), width)
    w_out = w_out_ref[...]
    copies = []
    for i in range(rows):
        norm = norm_ref[i]
        cotangent = jnp.transpose(cotangent_ref[i].astype(F32))
        projected = projections(wt_ref, norm, 5)
        out_gate = sigmoid(projected[4])
        gated = cotangent * out_gate
        slope_ref[i] = gated * (1.0 - out_gate)
        gated = gated.astype(BF16)
        gated_ref[i] = gated
        upstream = dot(w_out, gated, NN) * gain
        upstream = upstream - jnp.sum(upstream, axis=0, keepdims=True) * (1.0 / channels)
        for half in range(width // LANES):
            upstream_ref[half, pl.ds(i, channels, stride=rows), :] = upstream[
                :, half * LANES : (half + 1) * LANES
            ]
        mask = row_of_masks(length, i, rows, width)
        for side in range(2):
            value, gate = projected[2 * side], sigmoid(projected[2 * side + 1])
            masked = mask * gate
            factors[side][i, 0] = masked.astype(BF16)
            factors[side][i, 1] = (masked * value * (1.0 - gate)).astype(BF16)
    for n in range(5):
        copies.append(pltpu.make_async_copy(stages[n], outs[n], sems.at[n, 0]))
        copies[-1].start()
    for copy in copies:
        copy.wait()


def first_core():
    return lax.rem(lax.axis_index("dp").astype(jnp.int32), 2) == 0


def project_kernel(
    lengths_ref, pair_hbm, cotangent_hbm, w_hbm, gain_hbm, w_out_hbm, gain_out_hbm,
    send_hbm, norm_hbm, *rest,
):
    outs, stages = rest[:5], rest[5:10]
    pair_ref, cotangent_ref, w_ref, gain_ref, w_out_ref, gain_out_ref = rest[10:16]
    wt_ref, stage_ref, send_ref, norm_ref, sems, in_sems = rest[16:]
    rows, width, channels = pair_ref.shape
    length = lengths_ref[0]
    def fetch(source, target, n):
        return pltpu.make_async_copy(source, target, in_sems.at[n])

    first = [
        fetch(w_hbm, w_ref, 0),
        fetch(gain_hbm, gain_ref, 1),
        fetch(pair_hbm.at[: rows // 2], pair_ref.at[: rows // 2], 2),
        fetch(pair_hbm.at[rows // 2 :], pair_ref.at[rows // 2 :], 3),
    ]
    later = [
        fetch(cotangent_hbm, cotangent_ref, 4),
        fetch(w_out_hbm, w_out_ref, 5),
        fetch(gain_out_hbm, gain_out_ref, 6),
    ]
    for copy in first:
        copy.start()

    @pl.when(first_core())
    def _():
        for copy in later:
            copy.start()

    eye = identity(channels)
    first[0].wait()
    transposed_blocks(w_ref, wt_ref)
    first[1].wait()
    gain = wide(column(gain_ref[...], channels), width)
    peers = send_ref.shape[0]
    done = []
    for side in range(2):
        for i in range(rows):
            if side == 0:
                if 2 * i % rows == 0:
                    first[2 + 2 * i // rows].wait()
                hat, _ = norm_sublanes(jnp.transpose(pair_ref[i].astype(F32)))
                norm = (hat * gain).astype(BF16)
                norm_ref[i] = norm
            else:
                norm = norm_ref[i]
            blocks = slice(2 * side * channels, 2 * (side + 1) * channels)
            projected = dot(wt_ref[blocks], norm, NN)
            mask = row_of_masks(length, i, rows, width)
            value = mask * sigmoid(projected[channels:]) * projected[:channels]
            for half in range(width // LANES):
                stage_ref[side, half, pl.ds(i, channels, stride=rows), :] = value[
                    :, half * LANES : (half + 1) * LANES
                ]
        for half in range(width // LANES):
            send_ref[:, side, half] = (
                stage_ref[side, half].reshape(peers, -1, LANES).astype(BF16)
            )
        done.append(fetch(send_ref.at[:, side], send_hbm.at[:, side], 8 + side))
        done[-1].start()
        if side == 0:
            done.append(fetch(norm_ref, norm_hbm, 7))
            done[-1].start()

    @pl.when(first_core())
    def _():
        for copy in later:
            copy.wait()
        output_ahead(
            length, norm_ref, cotangent_ref, wt_ref, w_out_ref, gain_out_ref, outs, stages, sems
        )

    for copy in done:
        copy.wait()


def output_ahead_kernel(
    lengths_ref, norm_ref, cotangent_ref, w_ref, w_out_ref, gain_ref, *rest
):
    outs, stages = rest[5:10], rest[10:15]
    wt_ref, sems = rest[15:]

    @pl.when(jnp.logical_not(first_core()))
    def _():
        transposed_blocks(w_ref, wt_ref)
        output_ahead(
            lengths_ref[0], norm_ref, cotangent_ref, wt_ref, w_out_ref, gain_ref, outs, stages, sems
        )


def regroup(block, group):
    peers, _, lanes = block.shape
    block = block.astype(F32).reshape(peers, group, SUB, lanes)
    return [block[:, c].reshape(peers * SUB, lanes).astype(BF16) for c in range(group)]


def product_kernel(got_ref, send_ref, held_ref, stage_ref):
    peers, _, halves, packed, _ = got_ref.shape
    group = packed // SUB
    for side in range(2):
        for half in range(halves):
            for c, block in enumerate(regroup(got_ref[:, side, half], group)):
                held_ref[side, c, :, half * LANES : (half + 1) * LANES] = block
    for c in range(group):
        total = dot(held_ref[0, c], held_ref[1, c], NT)
        for out in range(halves):
            stage_ref[out, :, c * SUB : (c + 1) * SUB, :] = total[
                :, out * LANES : (out + 1) * LANES
            ].reshape(peers, SUB, LANES)
    for out in range(halves):
        send_ref[:, out] = stage_ref[out].astype(BF16)


def norm_blocks(block):
    product = block.astype(F32).reshape(-1, SUB, block.shape[-1])
    return norm_sublanes(product)


def output_back_kernel(got_ref, upstream_ref, send_ref):
    peers, halves, packed, lanes = got_ref.shape
    for half in range(halves):
        hat, inverse = norm_blocks(got_ref[:, half])
        upstream = upstream_ref[half].reshape(hat.shape)
        second = jnp.sum(upstream * hat, axis=0, keepdims=True) * (1.0 / hat.shape[0])
        grad = inverse * (upstream - hat * second)
        send_ref[:, half] = grad.reshape(peers, packed, lanes).astype(BF16)


def output_weights_kernel(
    got_ref, norm_ref, gated_ref, slope_ref, w_out_ref, gain_ref,
    gate_grad_ref, sums_ref, stage_ref,
):
    halves = got_ref.shape[1]
    rows, channels, _ = norm_ref.shape
    gain = column(gain_ref[...], channels)
    w_out_t = jnp.transpose(w_out_ref[...].astype(F32)).astype(BF16)
    for half in range(halves):
        hat, _ = norm_blocks(got_ref[:, half])
        stage_ref[half] = hat.reshape(-1, LANES)
    w_out_sum = jnp.zeros((channels, channels), F32)
    w_gate_sum = jnp.zeros((channels, channels), F32)
    for i in range(rows):
        for half in range(halves):
            lanes = slice(half * LANES, (half + 1) * LANES)
            hat = stage_ref[half, pl.ds(i, channels, stride=rows), :]
            prod_norm = (hat * gain).astype(BF16)
            update = dot(w_out_t, prod_norm, NN)
            gate_grad = (slope_ref[i, :, lanes] * update).astype(BF16)
            gate_grad_ref[i, :, lanes] = gate_grad
            w_out_sum = w_out_sum + dot(prod_norm, gated_ref[i, :, lanes], NT)
            w_gate_sum = w_gate_sum + dot(norm_ref[i, :, lanes], gate_grad, NT)
    sums_ref[0] = w_gate_sum
    sums_ref[1] = w_out_sum


def operands_back_kernel(got_ref, held_ref, send_hbm, stage_ref, send_ref, sems):
    peers, halves, packed, _ = got_ref.shape
    group = packed // SUB
    blocks = [regroup(got_ref[:, half], group) for half in range(halves)]
    grads = [jnp.concatenate([block[c] for block in blocks], axis=1) for c in range(group)]
    copies = []
    for side in (1, 0):
        for c in range(group):
            total = dot(grads[c], held_ref[1 - side, c], TN if side else NN)
            for out in range(halves):
                stage_ref[side, out, :, c * SUB : (c + 1) * SUB, :] = total[
                    :, out * LANES : (out + 1) * LANES
                ].reshape(peers, SUB, LANES)
        for out in range(halves):
            send_ref[:, side, out] = stage_ref[side, out].astype(BF16)
            copies.append(
                pltpu.make_async_copy(
                    send_ref.at[:, side, out], send_hbm.at[:, side, out], sems.at[side, out]
                )
            )
            copies[-1].start()
    for copy in copies:
        copy.wait()


def unpack(got_ref, stage_ref, side):
    for half in range(got_ref.shape[2]):
        stage_ref[half] = got_ref[:, side, half].astype(F32).reshape(-1, LANES)


def pieces_of(stage_ref, factors_ref, i, half, rows, channels):
    lanes = slice(half * LANES, (half + 1) * LANES)
    grad = stage_ref[half, pl.ds(i, channels, stride=rows), :]
    return jnp.concatenate(
        [(grad * factors_ref[i, n, :, lanes].astype(F32)).astype(BF16) for n in range(2)],
        axis=0,
    )


def side_weights(got_ref, factors_ref, norm_ref, parts_ref, stage_ref, side):
    rows, channels, _ = norm_ref.shape
    unpack(got_ref, stage_ref, side)
    total = jnp.zeros((channels, 2 * channels), F32)
    for i in range(rows):
        for half in range(got_ref.shape[2]):
            norm = norm_ref[i, :, half * LANES : (half + 1) * LANES]
            total = total + dot(norm, pieces_of(stage_ref, factors_ref, i, half, rows, channels), NT)
    for n in range(2):
        parts_ref[2 * side + n] = total[:, n * channels : (n + 1) * channels].astype(BF16)


def left_weights_kernel(got_ref, factors_ref, norm_ref, parts_ref, stage_ref):
    side_weights(got_ref, factors_ref, norm_ref, parts_ref, stage_ref, 0)


def right_weights_kernel(got_ref, factors_ref, norm_ref, sums_ref, left_ref, parts_ref, stage_ref):
    parts_ref[:2] = left_ref[...]
    side_weights(got_ref, factors_ref, norm_ref, parts_ref, stage_ref, 1)
    parts_ref[4] = sums_ref[0].astype(BF16)
    parts_ref[5] = sums_ref[1].astype(BF16)


def input_back_kernel(
    got_ref, left_ref, right_ref, gate_grad_ref, pair_ref, w_ref, gain_ref, out_ref, *stages
):
    rows, width, channels = pair_ref.shape
    eye = identity(channels)
    gain = wide(column(gain_ref[...], channels), width)
    for side in range(2):
        unpack(got_ref, stages[side], side)
    for i in range(rows):
        hat, inverse = norm_sublanes(jnp.transpose(pair_ref[i].astype(F32)))
        grad = dot(w_ref[:, 4 * channels :], gate_grad_ref[i], NN)
        for side in range(2):
            pieces = jnp.concatenate(
                [
                    pieces_of(stages[side], (left_ref, right_ref)[side], i, half, rows, channels)
                    for half in range(width // LANES)
                ],
                axis=1,
            )
            block = w_ref[:, 2 * side * channels : 2 * (side + 1) * channels]
            grad = grad + dot(block, pieces, NN)
        grad = grad * gain
        first = jnp.sum(grad, axis=0, keepdims=True) * (1.0 / channels)
        second = jnp.sum(grad * hat, axis=0, keepdims=True) * (1.0 / channels)
        grad = inverse * (grad - first - hat * second)
        out_ref[i] = jnp.transpose(grad).astype(BF16)


def fold_kernel(got_ref, send_ref):
    total = jnp.sum(got_ref[...].astype(F32), axis=0)
    send_ref[...] = jnp.broadcast_to(total[None], send_ref.shape).astype(send_ref.dtype)


def finish_kernel(
    factor, got_ref, w_ref, gain_in_ref, w_out_ref, gain_out_ref,
    w_in_grad_ref, gain_in_grad_ref, w_out_grad_ref, gain_out_grad_ref,
):
    channels = w_out_ref.shape[0]
    dots = jnp.zeros((channels, channels), F32)
    for n in range(5):
        total = got_ref[n].astype(F32) * factor
        lanes = slice(n * channels, (n + 1) * channels)
        w_in_grad_ref[:, lanes] = total
        dots = dots + total * w_ref[:, lanes].astype(F32)
    gain_in_grad_ref[...] = jnp.sum(jnp.transpose(dots), axis=0, keepdims=True) / gain_in_ref[...]
    total = got_ref[5].astype(F32) * factor
    w_out_grad_ref[...] = total
    dots = total * w_out_ref[...].astype(F32)
    gain_out_grad_ref[...] = jnp.sum(jnp.transpose(dots), axis=0, keepdims=True) / gain_out_ref[...]


def exchange(values, axis):
    return lax.all_to_all(values, axis, split_axis=0, concat_axis=0, tiled=True)


VMEM = pl.BlockSpec(memory_space=pltpu.VMEM)
SMEM = pl.BlockSpec(memory_space=pltpu.SMEM)
HBM = pl.BlockSpec(memory_space=pltpu.HBM)
COPIES = pltpu.SemaphoreType.DMA


def call(kernel, name, ins, outs, scratch=(), aliases=None, flops=10**9, grant=24):
    return pl.pallas_call(
        kernel,
        out_shape=[jax.ShapeDtypeStruct(shape, dtype) for shape, dtype, _ in outs],
        in_specs=ins,
        out_specs=[spec for _, _, spec in outs],
        scratch_shapes=[pltpu.VMEM(*item) if isinstance(item, tuple) else item for item in scratch],
        input_output_aliases=aliases or {},
        compiler_params=pltpu.CompilerParams(vmem_limit_bytes=grant * 2**20),
        cost_estimate=pl.CostEstimate(flops=flops, bytes_accessed=4 * 2**20, transcendentals=0),
        name=name,
    )


def per_device(pair, cotangent, lengths, w_in, gain_in, w_out, gain_out):
    _, rows, width, channels = pair.shape
    inner, outer = lax.axis_size("dap"), lax.axis_size("dp")
    halves, group = width // LANES, channels // inner
    packed = group * rows
    pair, cotangent = pair[0], cotangent[0]
    gain_in, gain_out = gain_in[None], gain_out[None]
    one_side, two_sides = (inner, halves, packed, LANES), (inner, 2, halves, packed, LANES)
    flat, square, row = (rows, channels, width), (channels, channels), (1, channels)
    mixed = (halves, channels * rows, LANES)

    ahead = [
        (mixed, F32),
        ((rows, 2, channels, width), BF16),
        (flat, BF16),
        (flat, F32),
        ((rows, 2, channels, width), BF16),
    ]
    ahead_outs = [(shape, dtype, HBM) for shape, dtype in ahead]
    transposed = ((5 * channels, channels), BF16)
    send, norm, *ahead_parts = call(
        project_kernel, "project", [SMEM] + [HBM] * 6,
        [(two_sides, BF16, HBM), (flat, BF16, HBM)] + ahead_outs,
        ahead
        + [
            ((rows, width, channels), BF16),
            ((rows, width, channels), BF16),
            ((channels, 5 * channels), BF16),
            (row, F32),
            (square, BF16),
            (row, F32),
            transposed,
            ((2,) + mixed, F32),
            (two_sides, BF16),
            (flat, BF16),
            COPIES((5, rows)),
            COPIES((10,)),
        ],
        grant=60,
    )(lengths, pair, cotangent, w_in, gain_in, w_out, gain_out)
    got_operands = exchange(send, "dap")
    upstream, left_factors, gated, slope, right_factors = call(
        output_ahead_kernel, "output_ahead", [SMEM] + [VMEM] * 5 + [HBM] * 5, ahead_outs,
        ahead + [transposed, COPIES((5, rows))],
        aliases={6 + n: n for n in range(5)}, flops=6 * 10**9, grant=60,
    )(lengths, norm, cotangent, w_in, w_out, gain_out, *ahead_parts)

    got_operands, upstream = lax.optimization_barrier((got_operands, upstream))
    send, held = call(
        product_kernel, "product", [VMEM],
        [(one_side, BF16, VMEM), ((2, group, width, width), BF16, VMEM)],
        [((halves, inner, packed, LANES), F32)],
    )(got_operands)
    got_product = exchange(send, "dap")

    (send,) = call(
        output_back_kernel, "output_back", [VMEM, VMEM], [(one_side, BF16, VMEM)],
    )(got_product, upstream)
    got_grad = exchange(send, "dap")
    gate_grad, sums = call(
        output_weights_kernel, "output_weights", [VMEM] * 6,
        [(flat, BF16, VMEM), ((2,) + square, F32, VMEM)],
        [(mixed, F32)], flops=4 * 10**9,
    )(got_product, norm, gated, slope, w_out, gain_out)

    (send,) = call(
        operands_back_kernel, "operands_back", [VMEM, VMEM], [(two_sides, BF16, HBM)],
        [((2, halves, inner, packed, LANES), F32), (two_sides, BF16), COPIES((2, halves))],
    )(got_grad, held)
    got_operand_grads = exchange(send, "dap")

    (left_parts,) = call(
        left_weights_kernel, "left_weights", [VMEM] * 3, [((2,) + square, BF16, VMEM)],
        [(mixed, F32)],
    )(got_operand_grads, left_factors, norm)
    (parts,) = call(
        right_weights_kernel, "right_weights", [VMEM] * 5, [((6,) + square, BF16, VMEM)],
        [(mixed, F32)],
    )(got_operand_grads, right_factors, norm, sums, left_parts)
    share = 6 * channels // inner
    got = exchange(parts.reshape(inner, share, channels), "dap")
    (pair_grad,) = call(
        input_back_kernel, "input_back", [VMEM] * 7, [((rows, width, channels), BF16, VMEM)],
        [(mixed, F32), (mixed, F32)], flops=6 * 10**9,
    )(got_operand_grads, left_factors, right_factors, gate_grad, pair, w_in, gain_in)
    (send,) = call(
        fold_kernel, "fold_inner", [VMEM], [((outer, share, channels), BF16, VMEM)]
    )(got)
    got = exchange(send, "dp")
    (send,) = call(
        fold_kernel, "fold_outer", [VMEM], [((inner, share, channels), BF16, VMEM)]
    )(got)
    got = exchange(send, "dap").reshape((6,) + square)
    factor = 1.0 / (width * math.sqrt(outer))

    def finish(*refs):
        finish_kernel(factor, *refs)

    w_in_grad, gain_in_grad, w_out_grad, gain_out_grad = call(
        finish, "finish", [VMEM] * 5,
        [
            ((channels, 5 * channels), F32, VMEM),
            (row, F32, VMEM),
            (square, F32, VMEM),
            (row, F32, VMEM),
        ],
    )(got, w_in, gain_in, w_out, gain_out)
    return (pair_grad[None], w_in_grad, gain_in_grad[0], w_out_grad, gain_out_grad[0])


def solution(mesh):
    in_specs = (P("dp", "dap", None, None), P("dp", "dap", None, None), P("dp"), P(), P(), P(), P())
    out_specs = (P("dp", "dap", None, None), P(), P(), P(), P())
    return jax.shard_map(
        per_device, mesh=mesh, in_specs=in_specs, out_specs=out_specs, check_vma=False
    )
```
